256 devices in a mesh: row: 8 (over z_lo, core), col: 32 (over z_hi, y, x).
Axes of the slice: x: 4, y: 4, z: 8 (z_hi: 2, z_lo: 4; z = z_hi * 4 + z_lo), core: 2. Of those that a mesh axis runs over, the one named last changes fastest.
Arguments:
- right_env: bfloat16 [8, 8, 9, 262144], P('row', None, None, 'col'), may hold values from -45 to 45
- left_env: bfloat16 [8, 8, 9, 262144], P('row', None, None, 'col'), may hold values from -45 to 45
- down_env: bfloat16 [8, 8, 9, 262144], P('row', None, None, 'col'), may hold values from -45 to 45
- up_env: bfloat16 [8, 8, 9, 262144], P('row', None, None, 'col'), may hold values from -45 to 45
- hamiltonian: float32 [9, 9], replicated, may hold values from -0.625 to 0.625
- parity: int32 [8], replicated, may hold values 0 or 1
Outputs:
- grad_right: bfloat16 [8, 8, 9, 262144], P('row', None, None, 'col')
- grad_left: bfloat16 [8, 8, 9, 262144], P('row', None, None, 'col')
- grad_down: bfloat16 [8, 8, 9, 262144], P('row', None, None, 'col')
- grad_up: bfloat16 [8, 8, 9, 262144], P('row', None, None, 'col')
- energy: float32 [], replicated
The draws below stay inside these ranges and needn't reach their ends.
All inputs are finite; a program needn't handle non-finite values.
Results may differ from the reference program's by a relative error of at most 0.0051.
Values may be sent and summed in bfloat16 or wider, within the bound.
A program may use at most 128 MiB of HBM per device.

```python
import math
import jax
import jax.numpy as jnp
from jax import lax

D = 8
CHI = 64
PAIRS = 9
NC = 8
NR = 8


def env_scaled(scale_key, values, low, high):
    site_key, leg_key = jax.random.split(scale_key)
    site_scale = jnp.exp(jax.random.uniform(site_key, (NR, NC, 1, 1, 1), jnp.float32, math.log(low), math.log(high)))
    leg_scale = jnp.exp(jax.random.uniform(leg_key, (1, 1, 1, CHI * CHI, 1), jnp.float32, math.log(low), math.log(high)))
    return (values * site_scale * leg_scale).reshape(NR, NC, PAIRS, CHI * CHI * D * D).astype(jnp.bfloat16)


def env_values(key, tag):
    key = jax.random.fold_in(key, tag)
    noise_key, scale_key = jax.random.split(key)
    values = jnp.clip(jax.random.normal(noise_key, (NR, NC, PAIRS, CHI * CHI, D * D), jnp.float32), -4.0, 4.0)
    return env_scaled(scale_key, values, 0.3, 3.0)


def draw_right_env(key, part):
    return env_values(key, 11)


def draw_left_env(key, part):
    return env_values(key, 23)


def draw_down_env(key, part):
    return env_values(key, 37)


def draw_up_env(key, part):
    return env_values(key, 41)


def with_ends(values, stream_key, low, largest):
    longest = values.shape.index(max(values.shape))
    spots = []
    for shift in (0, 1):
        where = [jax.random.randint(jax.random.fold_in(stream_key, axis), (), 0, length) for axis, length in enumerate(values.shape)]
        where[longest] = (where[longest] + shift) % values.shape[longest]
        spots.append(tuple(where))
    return values.at[spots[0]].set(low).at[spots[1]].set(largest)


def normal_values(key, extent, scale, bound, kind=jnp.bfloat16):
    array = jax.random.normal(key, extent, jnp.float32) * scale
    return jnp.minimum(jnp.maximum(array, -bound), bound).astype(kind)


def setup_inputs(seed: int = 0) -> dict:
    streams_of = jax.random.split(jax.random.key(seed), 7)
    right_env = draw_right_env(jax.random.fold_in(streams_of[6], 71), 0)
    left_env = draw_left_env(jax.random.fold_in(streams_of[6], 71), 0)
    down_env = draw_down_env(jax.random.fold_in(streams_of[6], 71), 0)
    up_env = draw_up_env(jax.random.fold_in(streams_of[6], 71), 0)
    hamiltonian = normal_values(streams_of[4], (PAIRS, PAIRS), (PAIRS * PAIRS) ** -0.5, 0.625, jnp.float32)
    parity = with_ends((jax.random.randint(streams_of[5], (D,), 0, 2) < 1).astype(jnp.int32), jax.random.fold_in(streams_of[5], 1), 0, 1)
    return {"right_env": right_env, "left_env": left_env, "down_env": down_env, "up_env": up_env, "hamiltonian": hamiltonian, "parity": parity}


def phys_parity():
    return jnp.minimum(jnp.arange(3, dtype=jnp.int32), 1)

def pair_signs(parity, leg_count):
    bond_dim = parity.shape[0]
    charge = phys_parity()
    exponent = charge[:, None, None, None] * parity[None, None, :, None] + charge[None, :, None, None] * parity[None, None, None, :]
    swap_sign = (1 - 2 * (exponent % 2)).astype(jnp.float32).reshape(9, 1, bond_dim * bond_dim)
    return jnp.broadcast_to(swap_sign, (9, leg_count, bond_dim * bond_dim)).reshape(9, leg_count * bond_dim * bond_dim)

def charge_mask():
    charge = phys_parity()
    ket_charge = charge[:, None, None, None] + charge[None, None, :, None]
    bra_charge = charge[None, :, None, None] + charge[None, None, None, :]
    return (ket_charge == bra_charge).astype(jnp.float32).reshape(9, 9)

def bond_terms(first_env, second, swap_sign, coupling, weight, valid_mask):
    signed = second * swap_sign.astype(jnp.bfloat16)
    density = jnp.einsum('rcpm,rcqm->rcpq', first_env.astype(jnp.float32), signed.astype(jnp.float32))
    frob_norm = jnp.sqrt(lax.optimization_barrier(jnp.mean(density * density, axis=(2, 3))) + 1e-06)
    trace_val = lax.optimization_barrier(jnp.sum(coupling * density, axis=(2, 3)))
    factor = valid_mask * weight
    energy = factor * trace_val / frob_norm
    entries = density.shape[2] * density.shape[3]
    bond_lam = factor[:, :, None, None] * (coupling / frob_norm[:, :, None, None] - (trace_val / (entries * frob_norm ** 3))[:, :, None, None] * density)
    bond_lam = bond_lam.astype(jnp.bfloat16)
    grad_first = jnp.einsum('rcpq,rcqm->rcpm', bond_lam.astype(jnp.float32), signed.astype(jnp.float32))
    grad_second = swap_sign * jnp.einsum('rcpq,rcpm->rcqm', bond_lam.astype(jnp.float32), first_env.astype(jnp.float32))
    return (energy, grad_first, grad_second)

def reference(right_env, left_env, down_env, up_env, hamiltonian, parity):
    row_total, col_total, pair_count, cut_width = right_env.shape
    bond_dim = parity.shape[0]
    swap_sign = pair_signs(parity, cut_width // (bond_dim * bond_dim))
    coupling = hamiltonian * charge_mask()
    col_pos = jnp.arange(col_total, dtype=jnp.int32).astype(jnp.float32)
    valid_cols = (jnp.arange(col_total, dtype=jnp.int32) < col_total - 1).astype(jnp.float32)[None, :]
    zero_column = jnp.zeros((1, 1, pair_count, cut_width), right_env.dtype)
    zero_grad = jnp.zeros((1, 1, pair_count, cut_width), jnp.float32)

    def take_row(source, row_index):
        return lax.dynamic_index_in_dim(source, row_index, 0, keepdims=True)

    def horizontal(row_index):
        first_env = take_row(right_env, row_index)
        second = jnp.concatenate([take_row(left_env, row_index)[:, 1:], zero_column], axis=1)
        weight = (1.0 + 2.0 * col_pos / col_total + row_index.astype(jnp.float32) / row_total)[None, :]
        return bond_terms(first_env, second, swap_sign, coupling, weight, valid_cols)

    def vertical(row_index):
        upper = jnp.clip(row_index, 0, row_total - 1).astype(jnp.int32)
        lower = jnp.clip(row_index + 1, 0, row_total - 1).astype(jnp.int32)
        first_env = take_row(down_env, upper)
        second = take_row(up_env, lower)
        inside = ((row_index >= 0) & (row_index < row_total - 1)).astype(jnp.float32)
        valid_mask = inside * jnp.ones((1, col_total), jnp.float32)
        weight = (1.0 + 2.0 * col_pos / col_total + row_index.astype(jnp.float32) / row_total)[None, :]
        return bond_terms(first_env, second, swap_sign, coupling, weight, valid_mask)

    def row_sums(row_index):
        energy_h, grad_a, grad_b = horizontal(row_index)
        energy_v, grad_c, grad_d = vertical(row_index)
        squares = jnp.sum(grad_a * grad_a) + jnp.sum(grad_b * grad_b) + jnp.sum(grad_c * grad_c) + jnp.sum(grad_d * grad_d)
        return (jnp.sum(energy_h) + jnp.sum(energy_v), squares)
    row_ids = jnp.arange(row_total, dtype=jnp.int32)
    energies, squares = lax.map(row_sums, row_ids)
    count = 4.0 * row_total * col_total * pair_count * cut_width
    grad_scale = 1.0 / jnp.sqrt(jnp.sum(squares) / count + 1e-06)

    def row_grads(row_index):
        energy_h, grad_r, partner = horizontal(row_index)
        grad_l = jnp.concatenate([zero_grad, partner[:, :col_total - 1]], axis=1)
        energy_v, grad_d, unused_up = vertical(row_index)
        energy_u, unused_down, grad_u = vertical(row_index - 1)
        return tuple(((piece[0] * grad_scale).astype(jnp.bfloat16) for piece in (grad_r, grad_l, grad_d, grad_u)))
    grad_right, grad_left, grad_down, grad_up = lax.map(row_grads, row_ids)
    energy = jnp.sum(energies) / col_total
    return (grad_right, grad_left, grad_down, grad_up, energy)
```

```python
import functools

import jax
import jax.numpy as jnp
from jax import lax
from jax.experimental import pallas as pl
from jax.experimental.pallas import tpu as pltpu
from jax.sharding import PartitionSpec as P

PAIRS = 9
SITES = 8
FLAT = PAIRS * SITES
BOND = 8
KINDS = 3 * PAIRS
LANES = 256
STEP = 1024
MESH = pl.DeviceIdType.MESH
HIGHEST = lax.Precision.HIGHEST
F32 = jnp.float32
BF16 = jnp.bfloat16


def iota(shape, dim):
    return lax.broadcasted_iota(jnp.int32, shape, dim)


def dot32(a, b):
    return jnp.dot(a, b, precision=HIGHEST, preferred_element_type=F32)


def dot16(a, b):
    return jnp.dot(a, b, preferred_element_type=F32)


def sign_tile(par):
    shape = (FLAT, 128)
    pair = iota(shape, 0) // SITES
    lane = iota(shape, 1) % (BOND * BOND)
    ket, bra = lane // BOND, lane % BOND
    par_ket = jnp.zeros(shape, jnp.int32)
    par_bra = jnp.zeros(shape, jnp.int32)
    for bond in range(BOND):
        value = par[bond]
        par_ket = jnp.where(ket == bond, value, par_ket)
        par_bra = jnp.where(bra == bond, value, par_bra)
    exponent = jnp.minimum(pair // 3, 1) * par_ket + jnp.minimum(pair % 3, 1) * par_bra
    return (1 - 2 * (exponent % 2)).astype(F32)


def compact(gram, shift):
    both = (FLAT, 2 * FLAT)
    row_site, col = iota(both, 0) % SITES, iota(both, 1)
    want = jnp.where(col < FLAT, row_site, row_site + shift)
    upper = jnp.where(col % SITES == want, gram[:FLAT, :], 0.0)
    spread = (2 * FLAT, LANES)
    source, lane = iota(spread, 0), iota(spread, 1)
    target = jnp.where(source < FLAT, PAIRS, 0) + (source % FLAT) // SITES
    upper = dot32(upper, (lane % KINDS == target).astype(F32))
    one = (FLAT, FLAT)
    lower = jnp.where(iota(one, 0) % SITES == iota(one, 1) % SITES, gram[FLAT:, FLAT:], 0.0)
    spread = (FLAT, LANES)
    source, lane = iota(spread, 0), iota(spread, 1)
    lower = dot32(lower, (lane % KINDS == 2 * PAIRS + source // SITES).astype(F32))
    keep = lane // KINDS == source // SITES
    upper = jnp.where(keep, upper, 0.0).reshape(PAIRS, SITES, LANES).sum(axis=0)
    lower = jnp.where(keep, lower, 0.0).reshape(PAIRS, SITES, LANES).sum(axis=0)
    if shift:
        lower = jnp.concatenate([lower[shift:], lower[:shift]], axis=0)
    return upper + lower


def lane_coupling(ham):
    shape = (PAIRS, PAIRS)
    p, q = iota(shape, 0), iota(shape, 1)

    def charge(state):
        return jnp.minimum(state, 1)

    same = charge(p // 3) + charge(q // 3) == charge(p % 3) + charge(q % 3)
    coupling = jnp.where(same, ham, 0.0)
    shape = (PAIRS, LANES)
    row, lane = iota(shape, 0), iota(shape, 1)
    wide = dot32(coupling, (lane % KINDS == row).astype(F32))
    return jnp.where(lane // KINDS == row, wide, 0.0).sum(axis=0, keepdims=True)


def finish(sums, coupling, factor):
    lane = iota((SITES, LANES), 1)
    density = jnp.where((lane % KINDS < PAIRS) & (lane < PAIRS * KINDS), sums, 0.0)
    entries = PAIRS * PAIRS
    norm = jnp.sqrt((density * density).sum(axis=1, keepdims=True) / entries + 1e-06)
    trace = (coupling * density).sum(axis=1, keepdims=True)
    energy = factor * trace / norm
    lam = factor * (coupling / norm - trace / (entries * norm**3) * density)
    return energy, lam.astype(BF16)


def block(rows, kind, shift, exact):
    shape = (FLAT, LANES)
    row, lane = iota(shape, 0), iota(shape, 1)
    tall = jnp.concatenate([rows] * PAIRS, axis=0)
    tall = jnp.where(lane // KINDS == row // SITES, tall, 0.0)
    shape = (LANES, FLAT)
    source, col = iota(shape, 0), iota(shape, 1)
    pick = (source % KINDS == kind * PAIRS + col // SITES).astype(F32)
    wide = dot32(tall, pick) if exact else dot16(tall.astype(BF16), pick.astype(BF16))
    shape = (FLAT, FLAT)
    return jnp.where(iota(shape, 1) % SITES == iota(shape, 0) % SITES + shift, wide, 0.0)


def block_t(rows, shift):
    if shift:
        rows = jnp.concatenate([rows[SITES - shift :], rows[: SITES - shift]], axis=0)
    shape = (FLAT, LANES)
    row, lane = iota(shape, 0), iota(shape, 1)
    tall = jnp.concatenate([rows] * PAIRS, axis=0)
    tall = jnp.where(lane % KINDS == row // SITES, tall, 0.0)
    shape = (LANES, FLAT)
    source, col = iota(shape, 0), iota(shape, 1)
    pick = source // KINDS == col // SITES
    wide = dot16(tall.astype(BF16), pick.astype(BF16))
    shape = (FLAT, FLAT)
    return jnp.where(iota(shape, 0) % SITES == iota(shape, 1) % SITES + shift, wide, 0.0)


def squares(sums, lam):
    weights = block(lam, 0, 0, False)
    first = block(sums, 1, 0, True)
    second = block(sums, 2, 0, True)
    total = dot32(weights, second) + dot32(first, weights)
    return (total * weights).sum()


def kernel(
    nx, ny, rows_total, cols_total,
    right, left, down, up, ham_hbm, par_hbm,
    g_right, g_left, g_down, g_up, energy,
    v_right, v_left, v_down, v_up, from_above, from_below, ham, par, sign,
    gram_h, gram_d, gram_u, buf_x, buf_y, buf_z, buf_above, buf_below, buf_row,
    load_sem, down_send, down_recv, up_send, up_recv,
    x_send, x_recv, y_send, y_recv, z_send, z_recv,
    above_send, above_recv, below_send, below_recv, row_send, row_recv,
):
    cut = right.shape[2]
    half = cut // 2
    steps = half // STEP
    row, col = lax.axis_index("row"), lax.axis_index("col")
    x, y, hi = col % nx, col // nx % ny, col // (nx * ny)
    plane = nx * ny
    has_above, has_below = row > 0, row < rows_total - 1

    pairs = (
        (ham_hbm, ham), (par_hbm, par), (right, v_right), (left, v_left), (down, v_down), (up, v_up),
    )
    loads = [
        pltpu.make_async_copy(source, target, load_sem.at[i]) for i, (source, target) in enumerate(pairs)
    ]
    for load in loads:
        load.start()

    same_x = [(row, hi * plane + y * nx + (x + i) % nx) for i in range(1, nx)]
    same_y = [(row, hi * plane + (y + i) % ny * nx + x) for i in range(1, ny)]
    partner = (row, (1 - hi) * plane + y * nx + x)
    mates = [((row + i) % rows_total, col) for i in range(1, rows_total)]
    here = y * nx + x
    aboves = [(row - 1, z * plane + here) for z in (0, 1)]
    belows = [(row + 1, z * plane + here) for z in (0, 1)]

    barrier = pltpu.get_barrier_semaphore()
    for device in same_x + same_y + [partner] + mates:
        pl.semaphore_signal(barrier, inc=1, device_id=device, device_id_type=MESH)

    @pl.when(has_above)
    def _():
        pl.semaphore_signal(barrier, inc=1, device_id=(row - 1, partner[1]), device_id_type=MESH)

    @pl.when(has_below)
    def _():
        pl.semaphore_signal(barrier, inc=1, device_id=(row + 1, partner[1]), device_id_type=MESH)

    count = len(same_x) + len(same_y) + 1 + len(mates)
    pl.semaphore_wait(barrier, count + has_above.astype(jnp.int32) + has_below.astype(jnp.int32))

    def span(start):
        return pl.ds(pl.multiple_of(start, STEP), STEP)

    def send_down(i):
        at = span(i * STEP)
        return pltpu.make_async_remote_copy(
            down.at[:, :, at], from_above.at[:, :, at], down_send.at[i], down_recv.at[i],
            device_id=(row + 1, col), device_id_type=MESH,
        )

    def up_start(i):
        return (i * STEP + half) % cut

    def send_up(i):
        at = span(up_start(i))
        return pltpu.make_async_remote_copy(
            up.at[:, :, at], from_below.at[:, :, at], up_send.at[i], up_recv.at[i],
            device_id=(row - 1, col), device_id_type=MESH,
        )

    def start_bulk(i):
        @pl.when(has_below)
        def _():
            send_down(i).start()

        @pl.when(has_above)
        def _():
            send_up(i).start()

    for i in range(steps):
        start_bulk(i)

    for load in loads[:2]:
        load.wait()
    tile = sign_tile(par)
    sign[...] = jnp.concatenate([tile] * (STEP // 128), axis=1)
    coupling = lane_coupling(ham[...])

    def flat(ref, at):
        return ref[:, :, at].reshape(FLAT, STEP)

    def signed(ref, at):
        return (flat(ref, at).astype(F32) * sign[...]).astype(BF16)

    def add_gram(gram, first, second):
        data = jnp.concatenate([first, second], axis=0)
        gram[...] += lax.dot_general(data, data, (((1,), (1,)), ((), ())), preferred_element_type=F32)

    for gram in (gram_h, gram_d, gram_u):
        gram[...] = jnp.zeros_like(gram)
    for load in loads[2:]:
        load.wait()

    @pl.loop(0, 2 * steps)
    def _(i):
        at = span(i * STEP)
        add_gram(gram_h, flat(v_right, at), signed(v_left, at))

    @pl.loop(0, steps)
    def _(i):
        at = span(i * STEP)

        @pl.when(has_above)
        def _():
            send_down(i).wait_recv()
            add_gram(gram_u, flat(from_above, at), signed(v_up, at))

        at_up = span(up_start(i))

        @pl.when(has_below)
        def _():
            send_up(i).wait_recv()
            add_gram(gram_d, flat(v_down, at_up), signed(from_below, at_up))
            send_down(i).wait_send()
            send_down(i + steps).start()

        @pl.when(has_above)
        def _():
            send_up(i).wait_send()
            send_up(i + steps).start()

    sums = jnp.concatenate(
        [compact(gram_h[...], 1), compact(gram_d[...], 0), compact(gram_u[...], 0)], axis=1
    )

    def gather(value, buf, me, devices, send, recv):
        buf[me] = value
        copies = [
            pltpu.make_async_remote_copy(
                buf.at[me], buf.at[me], send.at[i], recv.at[me], device_id=device, device_id_type=MESH
            )
            for i, device in enumerate(devices)
        ]
        for copy in copies:
            copy.start()
        return copies

    def arrived(buf, slot, recv):
        pltpu.make_async_remote_copy(
            buf.at[slot], buf.at[slot], recv.at[slot], recv.at[slot], device_id=(row, col), device_id_type=MESH
        ).wait_recv()

    def total(buf):
        value = buf[0]
        for i in range(1, buf.shape[0]):
            value = value + buf[i]
        return value

    sends = gather(sums, buf_x, x, same_x, x_send, x_recv)
    for i in range(1, nx):
        arrived(buf_x, (x + i) % nx, x_recv)
    sums = total(buf_x)
    sends += gather(sums, buf_y, y, same_y, y_send, y_recv)
    for i in range(1, ny):
        arrived(buf_y, (y + i) % ny, y_recv)
    sums = total(buf_y)

    sends += gather(sums, buf_z, hi, [partner], z_send, z_recv)

    def to_below(z):
        return pltpu.make_async_remote_copy(
            buf_z.at[hi, :, pl.ds(LANES, LANES)], buf_above.at[hi],
            below_send.at[z], above_recv.at[hi], device_id=belows[z], device_id_type=MESH,
        )

    def to_above(z):
        return pltpu.make_async_remote_copy(
            buf_z.at[hi, :, pl.ds(2 * LANES, LANES)], buf_below.at[hi],
            above_send.at[z], below_recv.at[hi], device_id=aboves[z], device_id_type=MESH,
        )

    @pl.when(has_below)
    def _():
        for z in (0, 1):
            to_below(z).start()

    @pl.when(has_above)
    def _():
        for z in (0, 1):
            to_above(z).start()

    arrived(buf_z, 1 - hi, z_recv)

    @pl.when(has_above)
    def _():
        for z in (0, 1):
            arrived(buf_above, z, above_recv)

    @pl.when(has_below)
    def _():
        for z in (0, 1):
            arrived(buf_below, z, below_recv)

    @pl.when(jnp.logical_not(has_above))
    def _():
        buf_above[...] = jnp.zeros_like(buf_above)

    @pl.when(jnp.logical_not(has_below))
    def _():
        buf_below[...] = jnp.zeros_like(buf_below)

    sums = total(buf_z)
    sums_h = sums[:, :LANES]
    sums_v = sums[:, LANES : 2 * LANES] + total(buf_below)
    sums_w = total(buf_above) + sums[:, 2 * LANES :]

    site = iota((SITES, 1), 0).astype(F32)
    weight = 1.0 + 2.0 * site / SITES + row.astype(F32) / rows_total
    weight_above = 1.0 + 2.0 * site / SITES + (row - 1).astype(F32) / rows_total
    energy_h, lam_h = finish(sums_h, coupling, jnp.where(site < SITES - 1, weight, 0.0))
    energy_v, lam_v = finish(sums_v, coupling, weight * has_below.astype(F32))
    _, lam_w = finish(sums_w, coupling, weight_above * has_above.astype(F32))
    lam_h, lam_v, lam_w = lam_h.astype(F32), lam_v.astype(F32), lam_w.astype(F32)
    square = squares(sums_h, lam_h) + squares(sums_v, lam_v)
    energies = (energy_h + energy_v).sum()
    lane = iota((SITES, 128), 1)
    message = jnp.where(lane == 0, square, jnp.where(lane == 1, energies, 0.0))
    sends += gather(message, buf_row, row, mates, row_send, row_recv)

    to_right = block(lam_h, 0, 1, False).astype(BF16)
    to_left = block_t(lam_h, 1).astype(BF16)
    to_down = block(lam_v, 0, 0, False).astype(BF16)
    to_up = block_t(lam_w, 0).astype(BF16)

    for i in range(1, rows_total):
        arrived(buf_row, (row + i) % rows_total, row_recv)
    message = total(buf_row)
    square = jnp.maximum(message[:1, :1], 0.0)
    scale = 1.0 / jnp.sqrt(square / (4.0 * rows_total * FLAT * cols_total * cut) + 1e-06)
    energy[...] = message[:1, 1:2] / SITES

    def put(ref, at, value):
        ref[:, :, at] = value.astype(BF16).reshape(PAIRS, SITES, STEP)

    @pl.loop(0, 2 * steps)
    def _(i):
        at = span(i * STEP)
        put(g_right, at, dot16(to_right, signed(v_left, at)) * scale)
        put(g_left, at, dot16(to_left, flat(v_right, at)) * (sign[...] * scale))

    def grad_down(at):
        put(g_down, at, dot16(to_down, signed(from_below, at)) * scale)

    def grad_up(at):
        put(g_up, at, dot16(to_up, flat(from_above, at)) * (sign[...] * scale))

    @pl.loop(0, 2 * steps)
    def _(i):
        at, at_up = span(i * STEP), span(up_start(i))

        @pl.when(has_above)
        def _():
            @pl.when(i >= steps)
            def _():
                send_down(i).wait_recv()

            grad_up(at)

        @pl.when(has_below)
        def _():
            @pl.when(i >= steps)
            def _():
                send_up(i).wait_recv()

            grad_down(at_up)

    @pl.when(jnp.logical_not(has_above))
    def _():
        g_up[...] = jnp.zeros_like(g_up)

    @pl.when(jnp.logical_not(has_below))
    def _():
        g_down[...] = jnp.zeros_like(g_down)

    @pl.when(has_below)
    def _():
        for i in range(steps, 2 * steps):
            send_down(i).wait_send()
        for z in (0, 1):
            to_below(z).wait_send()

    @pl.when(has_above)
    def _():
        for i in range(steps, 2 * steps):
            send_up(i).wait_send()
        for z in (0, 1):
            to_above(z).wait_send()

    for copy in sends:
        copy.wait_send()


def shards(nx, ny, cols_total, right_env, left_env, down_env, up_env, hamiltonian, parity):
    rows_total = lax.axis_size("row")
    cut = right_env.shape[3]
    chunks = cut // STEP
    envs = [e.transpose(0, 2, 1, 3).reshape(PAIRS, SITES, cut) for e in (right_env, left_env, down_env, up_env)]
    env = (PAIRS, SITES, cut)
    dma = pltpu.SemaphoreType.DMA
    hbm_spec = pl.BlockSpec(memory_space=pltpu.HBM)
    vmem_spec = pl.BlockSpec(memory_space=pltpu.VMEM)
    outs = pl.pallas_call(
        functools.partial(kernel, nx, ny, rows_total, cols_total),
        out_shape=[pltpu.VMEM(env, BF16)] * 4 + [jax.ShapeDtypeStruct((1, 1), F32)],
        in_specs=[hbm_spec] * 6,
        out_specs=[vmem_spec] * 5,
        scratch_shapes=[pltpu.VMEM(env, BF16)] * 6
        + [
            pltpu.VMEM((PAIRS, PAIRS), F32),
            pltpu.SMEM((BOND,), jnp.int32),
            pltpu.VMEM((FLAT, STEP), F32),
        ]
        + [pltpu.VMEM((2 * FLAT, 2 * FLAT), F32)] * 3
        + [
            pltpu.VMEM((nx, SITES, 3 * LANES), F32),
            pltpu.VMEM((ny, SITES, 3 * LANES), F32),
            pltpu.VMEM((2, SITES, 3 * LANES), F32),
            pltpu.VMEM((2, SITES, LANES), F32),
            pltpu.VMEM((2, SITES, LANES), F32),
            pltpu.VMEM((rows_total, SITES, 128), F32),
            dma((6,)),
            dma((chunks,)), dma((chunks,)), dma((chunks,)), dma((chunks,)),
            dma((nx,)), dma((nx,)), dma((ny,)), dma((ny,)), dma((2,)), dma((2,)),
            dma((2,)), dma((2,)), dma((2,)), dma((2,)), dma((rows_total,)), dma((rows_total,)),
        ],
        compiler_params=pltpu.CompilerParams(
            collective_id=0, has_side_effects=True, vmem_limit_bytes=40 * 1024 * 1024
        ),
    )(*[pltpu.with_memory_space_constraint(a, pltpu.HBM) for a in (*envs, hamiltonian, parity)])
    grads = [g.reshape(1, PAIRS, SITES, cut).transpose(0, 2, 1, 3) for g in outs[:4]]
    return (*grads, outs[4].reshape(()))


def solution(mesh):
    spec = P("row", None, None, "col")
    side = 4
    return jax.shard_map(
        functools.partial(shards, side, mesh.shape["col"] // (2 * side), mesh.shape["col"]),
        mesh=mesh,
        in_specs=(spec, spec, spec, spec, P(), P()),
        out_specs=(spec, spec, spec, spec, P()),
        check_vma=False,
    )
```

```python
import functools

import jax
import jax.numpy as jnp
from jax import lax
from jax.experimental import pallas as pl
from jax.experimental.pallas import tpu as pltpu
from jax.sharding import PartitionSpec as P

PAIRS = 9
SITES = 8
FLAT = PAIRS * SITES
BOND = 8
LANES = 128
STEP = 1024
WRITES = 4
MESH = pl.DeviceIdType.MESH
HIGHEST = lax.Precision.HIGHEST
F32 = jnp.float32
BF16 = jnp.bfloat16


def iota(shape, dim):
    return lax.broadcasted_iota(jnp.int32, shape, dim)


def dot32(a, b):
    return jnp.dot(a, b, precision=HIGHEST, preferred_element_type=F32)


def dot16(a, b):
    return jnp.dot(a, b, preferred_element_type=F32)


def sign_tile(par):
    shape = (FLAT, 128)
    pair = iota(shape, 0) // SITES
    lane = iota(shape, 1) % (BOND * BOND)
    ket, bra = lane // BOND, lane % BOND
    par_ket = jnp.zeros(shape, jnp.int32)
    par_bra = jnp.zeros(shape, jnp.int32)
    for bond in range(BOND):
        value = par[bond]
        par_ket = jnp.where(ket == bond, value, par_ket)
        par_bra = jnp.where(bra == bond, value, par_bra)
    exponent = jnp.minimum(pair // 3, 1) * par_ket + jnp.minimum(pair % 3, 1) * par_bra
    return (1 - 2 * (exponent % 2)).astype(F32)


def compact(grams, shifts):
    square = (FLAT, FLAT)
    row_site, col_site = iota(square, 0) % SITES, iota(square, 1) % SITES
    rows = jnp.concatenate(
        [jnp.where(col_site == row_site + shift, gram, 0.0) for gram, shift in zip(grams, shifts, strict=True)],
        axis=0,
    )
    spread = (FLAT, LANES)
    source, lane = iota(spread, 0), iota(spread, 1)
    wide = dot32(rows, (lane % PAIRS == source // SITES).astype(F32))
    keep = lane // PAIRS == source // SITES
    out = []
    for i in range(len(grams)):
        part = jnp.where(keep, wide[i * FLAT : (i + 1) * FLAT], 0.0)
        out.append(part.reshape(PAIRS, SITES, LANES).sum(axis=0))
    return out


def rolled(rows, shift):
    shift %= SITES
    if not shift:
        return rows
    return jnp.concatenate([rows[shift:], rows[:shift]], axis=0)


def lane_coupling(ham):
    shape = (PAIRS, PAIRS)
    p, q = iota(shape, 0), iota(shape, 1)

    def charge(state):
        return jnp.minimum(state, 1)

    same = charge(p // 3) + charge(q // 3) == charge(p % 3) + charge(q % 3)
    coupling = jnp.where(same, ham, 0.0)
    shape = (PAIRS, LANES)
    row, lane = iota(shape, 0), iota(shape, 1)
    wide = dot32(coupling, (lane % PAIRS == row).astype(F32))
    return jnp.where(lane // PAIRS == row, wide, 0.0).sum(axis=0, keepdims=True)


def finish(density, coupling, factor):
    entries = PAIRS * PAIRS
    norm = jnp.sqrt((density * density).sum(axis=1, keepdims=True) / entries + 1e-06)
    trace = (coupling * density).sum(axis=1, keepdims=True)
    energy = factor * trace / norm
    lam = factor * (coupling / norm - trace / (entries * norm**3) * density)
    return energy, lam.astype(BF16).astype(F32)


def block(rows, shift, transposed, exact):
    shape = (FLAT, LANES)
    row, lane = iota(shape, 0), iota(shape, 1)
    tall = jnp.concatenate([rolled(rows, -shift) if transposed else rows] * PAIRS, axis=0)
    mine = lane % PAIRS if transposed else lane // PAIRS
    tall = jnp.where(mine == row // SITES, tall, 0.0)
    shape = (LANES, FLAT)
    source, col = iota(shape, 0), iota(shape, 1)
    other = source // PAIRS if transposed else source % PAIRS
    pick = (other == col // SITES).astype(F32)
    wide = dot32(tall, pick) if exact else dot16(tall.astype(BF16), pick.astype(BF16))
    shape = (FLAT, FLAT)
    row_site, col_site = iota(shape, 0) % SITES, iota(shape, 1) % SITES
    hit = row_site == col_site + shift if transposed else col_site == row_site + shift
    return jnp.where(hit, wide, 0.0)


def thirds(value):
    high = value.astype(BF16)
    rest = value - high.astype(F32)
    middle = rest.astype(BF16)
    return high, middle, (rest - middle.astype(F32)).astype(BF16)


def kernel(
    nx, ny, rows_total,
    right, left, down, up, ham_hbm, par_hbm,
    g_right, g_left, g_down, g_up, totals,
    v_right, v_left, v_down, v_up, from_above, from_below, ham, par, sign,
    gram_h, gram_dd, gram_uu, gram_d, gram_u, early_x, early_y, early_z, late_x, late_y, late_z,
    late_above, late_below, buf_row,
    load_sem, down_send, down_recv, up_send, up_recv,
    ex_send, ex_recv, ey_send, ey_recv, ez_send, ez_recv,
    x_send, x_recv, y_send, y_recv, z_send, z_recv,
    above_send, above_recv, below_send, below_recv, row_send, row_recv,
):
    cut = right.shape[2]
    half = cut // 2
    steps = half // STEP
    row, col = lax.axis_index("row"), lax.axis_index("col")
    x, y, hi = col % nx, col // nx % ny, col // (nx * ny)
    plane = nx * ny
    has_above, has_below = row > 0, row < rows_total - 1

    pairs = (
        (ham_hbm, ham), (par_hbm, par), (right, v_right), (left, v_left), (down, v_down), (up, v_up),
    )
    loads = [
        pltpu.make_async_copy(source, target, load_sem.at[i]) for i, (source, target) in enumerate(pairs)
    ]
    for load in loads:
        load.start()

    same_x = [(row, hi * plane + y * nx + (x + i) % nx) for i in range(1, nx)]
    same_y = [(row, hi * plane + (y + i) % ny * nx + x) for i in range(1, ny)]
    partner = (row, (1 - hi) * plane + y * nx + x)
    mates = [((row + i) % rows_total, col) for i in range(1, rows_total)]
    here = y * nx + x
    aboves = [(row - 1, z * plane + here) for z in (0, 1)]
    belows = [(row + 1, z * plane + here) for z in (0, 1)]

    barrier = pltpu.get_barrier_semaphore()
    for device in same_x + same_y + [partner] + mates:
        pl.semaphore_signal(barrier, inc=1, device_id=device, device_id_type=MESH)

    @pl.when(has_above)
    def _():
        pl.semaphore_signal(barrier, inc=1, device_id=(row - 1, partner[1]), device_id_type=MESH)

    @pl.when(has_below)
    def _():
        pl.semaphore_signal(barrier, inc=1, device_id=(row + 1, partner[1]), device_id_type=MESH)

    count = len(same_x) + len(same_y) + 1 + len(mates)
    pl.semaphore_wait(barrier, count + has_above.astype(jnp.int32) + has_below.astype(jnp.int32))

    def span(start):
        return pl.ds(pl.multiple_of(start, STEP), STEP)

    def send_down(i):
        at = span(i * STEP)
        return pltpu.make_async_remote_copy(
            down.at[:, :, at], from_above.at[:, :, at], down_send.at[i], down_recv.at[i],
            device_id=(row + 1, col), device_id_type=MESH,
        )

    def up_start(i):
        return (i * STEP + half) % cut

    def send_up(i):
        at = span(up_start(i))
        return pltpu.make_async_remote_copy(
            up.at[:, :, at], from_below.at[:, :, at], up_send.at[i], up_recv.at[i],
            device_id=(row - 1, col), device_id_type=MESH,
        )

    for i in range(steps):

        @pl.when(has_below)
        def _(i=i):
            send_down(i).start()

        @pl.when(has_above)
        def _(i=i):
            send_up(i).start()

    for load in loads[:2]:
        load.wait()
    tile = sign_tile(par).astype(BF16)
    sign[...] = jnp.concatenate([tile] * (STEP // 128), axis=1)
    coupling = lane_coupling(ham[...])

    def flat(ref, at):
        return ref[:, :, at].reshape(FLAT, STEP)

    def signed(ref, at):
        value = flat(ref, at) * sign[...]
        ref[:, :, at] = value.reshape(PAIRS, SITES, STEP)
        return value

    def product(first, second):
        return lax.dot_general(first, second, (((1,), (1,)), ((), ())), preferred_element_type=F32)

    for gram in (gram_h, gram_dd, gram_uu, gram_d, gram_u):
        gram[...] = jnp.zeros_like(gram)
    for load in loads[2:]:
        load.wait()

    @pl.loop(0, 2 * steps)
    def _(i):
        at = span(i * STEP)
        data = jnp.concatenate([flat(v_right, at), signed(v_left, at)], axis=0)
        gram_h[...] += product(data, data)
        data = flat(v_down, at)
        gram_dd[...] += product(data, data)
        data = signed(v_up, at)
        gram_uu[...] += product(data, data)

    def gather(value, buf, me, devices, send, recv):
        buf[me] = value
        copies = [
            pltpu.make_async_remote_copy(
                buf.at[me], buf.at[me], send.at[i], recv.at[me], device_id=device, device_id_type=MESH
            )
            for i, device in enumerate(devices)
        ]
        for copy in copies:
            copy.start()
        return copies

    def arrived(buf, slot, recv):
        pltpu.make_async_remote_copy(
            buf.at[slot], buf.at[slot], recv.at[slot], recv.at[slot], device_id=(row, col), device_id_type=MESH
        ).wait_recv()

    def all_arrived(buf, me, recv):
        count = buf.shape[0]
        for i in range(1, count):
            arrived(buf, (me + i) % count, recv)
        value = buf[0]
        for i in range(1, count):
            value = value + buf[i]
        return value

    early = compact(
        [gram_h[:FLAT, FLAT:], gram_h[:FLAT, :FLAT], gram_h[FLAT:, FLAT:], gram_dd[...], gram_uu[...]],
        [1, 0, 0, 0, 0],
    )
    early[2] = rolled(early[2], 1)
    sends = gather(jnp.concatenate(early, axis=1), early_x, x, same_x, ex_send, ex_recv)

    def meet(i):
        at, at_up = span(i * STEP), span(up_start(i))

        @pl.when(has_above)
        def _():
            send_down(i).wait_recv()
            gram_u[...] += product(flat(from_above, at), flat(v_up, at))

        @pl.when(has_below)
        def _():
            send_up(i).wait_recv()
            gram_d[...] += product(flat(v_down, at_up), signed(from_below, at_up))
            send_down(i).wait_send()
            send_down(i + steps).start()

        @pl.when(has_above)
        def _():
            send_up(i).wait_send()
            send_up(i + steps).start()

    for i in range(steps // 2):
        meet(i)
    early = all_arrived(early_x, x, ex_recv)
    sends += gather(early, early_y, y, same_y, ey_send, ey_recv)
    for i in range(steps // 2, steps):
        meet(i)

    late = jnp.concatenate(compact([gram_d[...], gram_u[...]], [0, 0]), axis=1)
    sends += gather(late, late_x, x, same_x, x_send, x_recv)
    early = all_arrived(early_y, y, ey_recv)
    sends += gather(early, early_z, hi, [partner], ez_send, ez_recv)
    late = all_arrived(late_x, x, x_recv)
    sends += gather(late, late_y, y, same_y, y_send, y_recv)
    early = all_arrived(early_z, hi, ez_recv)
    density_h, rr, ll, dd, uu = [early[:, i * LANES : (i + 1) * LANES] for i in range(5)]
    rr, ll, dd, uu = [thirds(block(g, 0, False, True)) for g in (rr, ll, dd, uu)]
    site = iota((SITES, 1), 0).astype(F32)
    weight = 1.0 + 2.0 * site / SITES + row.astype(F32) / rows_total
    weight_above = 1.0 + 2.0 * site / SITES + (row - 1).astype(F32) / rows_total
    energy_h, lam_h = finish(density_h, coupling, jnp.where(site < SITES - 1, weight, 0.0))
    weights = block(lam_h, 0, False, False)
    small = weights.astype(BF16)
    total_h = sum(dot16(small, g) for g in ll) + sum(dot16(g, small) for g in rr)
    square_h = (total_h * weights).sum()
    to_right = block(lam_h, 1, False, False).astype(BF16)
    to_left = block(lam_h, 1, True, False).astype(BF16)
    late = all_arrived(late_y, y, y_recv)

    sends += gather(late, late_z, hi, [partner], z_send, z_recv)

    def to_below(z):
        return pltpu.make_async_remote_copy(
            late_z.at[hi, :, pl.ds(0, LANES)], late_above.at[hi],
            below_send.at[z], above_recv.at[hi], device_id=belows[z], device_id_type=MESH,
        )

    def to_above(z):
        return pltpu.make_async_remote_copy(
            late_z.at[hi, :, pl.ds(LANES, LANES)], late_below.at[hi],
            above_send.at[z], below_recv.at[hi], device_id=aboves[z], device_id_type=MESH,
        )

    @pl.when(has_below)
    def _():
        for z in (0, 1):
            to_below(z).start()

    @pl.when(has_above)
    def _():
        for z in (0, 1):
            to_above(z).start()

    def put(ref, at, value):
        ref[:, :, at] = value.reshape(PAIRS, SITES, STEP)

    @pl.loop(0, 2 * steps)
    def _(i):
        at = span(i * STEP)
        put(g_right, at, dot16(to_right, flat(v_left, at)))
        put(g_left, at, dot16(to_left, flat(v_right, at)) * sign[...].astype(F32))

    late = all_arrived(late_z, hi, z_recv)

    @pl.when(has_above)
    def _():
        for z in (0, 1):
            arrived(late_above, z, above_recv)

    @pl.when(has_below)
    def _():
        for z in (0, 1):
            arrived(late_below, z, below_recv)

    @pl.when(jnp.logical_not(has_above))
    def _():
        late_above[...] = jnp.zeros_like(late_above)

    @pl.when(jnp.logical_not(has_below))
    def _():
        late_below[...] = jnp.zeros_like(late_below)

    density_v = late[:, :LANES] + (late_below[0] + late_below[1])
    density_w = (late_above[0] + late_above[1]) + late[:, LANES:]
    energy_v, lam_v = finish(density_v, coupling, weight * has_below.astype(F32))
    _, lam_w = finish(density_w, coupling, weight_above * has_above.astype(F32))
    weights_v, weights_w = block(lam_v, 0, False, False), block(lam_w, 0, False, False)
    to_down, small = weights_v.astype(BF16), weights_w.astype(BF16)
    total_v = sum(dot16(g, to_down) for g in dd)
    total_w = sum(dot16(small, g) for g in uu)
    square = square_h + (total_v * weights_v + total_w * weights_w).sum()
    energies = (energy_h + energy_v).sum()
    lane = iota((SITES, LANES), 1)
    message = jnp.where(lane == 0, square, jnp.where(lane == 1, energies, 0.0))
    sends += gather(message, buf_row, row, mates, row_send, row_recv)
    to_up = block(lam_w, 0, True, False).astype(BF16)

    @pl.loop(0, 2 * steps)
    def _(i):
        at, at_up = span(i * STEP), span(up_start(i))

        @pl.when(has_above)
        def _():
            @pl.when(i >= steps)
            def _():
                send_down(i).wait_recv()

            put(g_up, at, dot16(to_up, flat(from_above, at)) * sign[...].astype(F32))

        @pl.when(has_below)
        def _():
            @pl.when(i >= steps)
            def _():
                send_up(i).wait_recv()
                signed(from_below, at_up)

            put(g_down, at_up, dot16(to_down, flat(from_below, at_up)))

    @pl.when(jnp.logical_not(has_above))
    def _():
        g_up[...] = jnp.zeros_like(g_up)

    @pl.when(jnp.logical_not(has_below))
    def _():
        g_down[...] = jnp.zeros_like(g_down)

    @pl.when(has_below)
    def _():
        for i in range(steps, 2 * steps):
            send_down(i).wait_send()
        for z in (0, 1):
            to_below(z).wait_send()

    @pl.when(has_above)
    def _():
        for i in range(steps, 2 * steps):
            send_up(i).wait_send()
        for z in (0, 1):
            to_above(z).wait_send()

    totals[...] = all_arrived(buf_row, row, row_recv)
    for copy in sends:
        copy.wait_send()


def scale_kernel(
    count, totals, raw_right, raw_left, raw_down, raw_up,
    g_right, g_left, g_down, g_up, energy, o_right, o_left, o_down, o_up, sems,
):
    message = totals[...]
    square = jnp.maximum(message[:1, :1], 0.0)
    scale = 1.0 / jnp.sqrt(square / count + 1e-06)
    energy[...] = message[:1, 1:2] / SITES
    cut = raw_right.shape[2]
    width = cut // WRITES
    arrays = (
        (raw_right, o_right, g_right), (raw_left, o_left, g_left), (raw_down, o_down, g_down), (raw_up, o_up, g_up),
    )
    copies = []
    for a, (raw, out, target) in enumerate(arrays):
        for i in range(WRITES):
            at = pl.ds(i * width, width)

            @pl.loop(0, PAIRS)
            def _(p, raw=raw, out=out, at=at):
                out[p, :, at] = (raw[p, :, at] * scale).astype(BF16)

            copies.append(pltpu.make_async_copy(out.at[:, :, at], target.at[:, :, at], sems.at[a, i]))
            copies[-1].start()
    for copy in copies:
        copy.wait()


def shards(nx, ny, cols_total, right_env, left_env, down_env, up_env, hamiltonian, parity):
    rows_total = lax.axis_size("row")
    cut = right_env.shape[3]
    chunks = cut // STEP
    envs = [e.transpose(0, 2, 1, 3).reshape(PAIRS, SITES, cut) for e in (right_env, left_env, down_env, up_env)]
    env = (PAIRS, SITES, cut)
    dma = pltpu.SemaphoreType.DMA
    hbm_spec = pl.BlockSpec(memory_space=pltpu.HBM)
    vmem_spec = pl.BlockSpec(memory_space=pltpu.VMEM)
    square = pltpu.VMEM((FLAT, FLAT), F32)
    early, late = 5 * LANES, 2 * LANES
    raw = pl.pallas_call(
        functools.partial(kernel, nx, ny, rows_total),
        out_shape=[pltpu.VMEM(env, F32)] * 4 + [pltpu.VMEM((SITES, LANES), F32)],
        in_specs=[hbm_spec] * 6,
        out_specs=[vmem_spec] * 5,
        scratch_shapes=[pltpu.VMEM(env, BF16)] * 6
        + [
            pltpu.VMEM((PAIRS, PAIRS), F32),
            pltpu.SMEM((BOND,), jnp.int32),
            pltpu.VMEM((FLAT, STEP), BF16),
            pltpu.VMEM((2 * FLAT, 2 * FLAT), F32),
            square, square, square, square,
            pltpu.VMEM((nx, SITES, early), F32),
            pltpu.VMEM((ny, SITES, early), F32),
            pltpu.VMEM((2, SITES, early), F32),
            pltpu.VMEM((nx, SITES, late), F32),
            pltpu.VMEM((ny, SITES, late), F32),
            pltpu.VMEM((2, SITES, late), F32),
            pltpu.VMEM((2, SITES, LANES), F32),
            pltpu.VMEM((2, SITES, LANES), F32),
            pltpu.VMEM((rows_total, SITES, LANES), F32),
            dma((6,)),
            dma((chunks,)), dma((chunks,)), dma((chunks,)), dma((chunks,)),
            dma((nx,)), dma((nx,)), dma((ny,)), dma((ny,)), dma((2,)), dma((2,)),
            dma((nx,)), dma((nx,)), dma((ny,)), dma((ny,)), dma((2,)), dma((2,)),
            dma((2,)), dma((2,)), dma((2,)), dma((2,)), dma((rows_total,)), dma((rows_total,)),
        ],
        compiler_params=pltpu.CompilerParams(
            collective_id=0, has_side_effects=True, vmem_limit_bytes=32 * 1024 * 1024
        ),
    )(*[pltpu.with_memory_space_constraint(a, pltpu.HBM) for a in (*envs, hamiltonian, parity)])
    count = 4.0 * rows_total * FLAT * cols_total * cut
    outs = pl.pallas_call(
        functools.partial(scale_kernel, count),
        out_shape=[jax.ShapeDtypeStruct(env, BF16)] * 4 + [jax.ShapeDtypeStruct((1, 1), F32)],
        in_specs=[vmem_spec] * 5,
        out_specs=[hbm_spec] * 4 + [vmem_spec],
        scratch_shapes=[pltpu.VMEM(env, BF16)] * 4 + [dma((4, WRITES))],
        compiler_params=pltpu.CompilerParams(vmem_limit_bytes=16 * 1024 * 1024),
    )(*[pltpu.with_memory_space_constraint(a, pltpu.VMEM) for a in (raw[4], *raw[:4])])
    grads = [g.reshape(1, PAIRS, SITES, cut).transpose(0, 2, 1, 3) for g in outs[:4]]
    return (*grads, outs[4].reshape(()))


def solution(mesh):
    spec = P("row", None, None, "col")
    side = 4
    return jax.shard_map(
        functools.partial(shards, side, mesh.shape["col"] // (2 * side), mesh.shape["col"]),
        mesh=mesh,
        in_specs=(spec, spec, spec, spec, P(), P()),
        out_specs=(spec, spec, spec, spec, P()),
        check_vma=False,
    )
```

```python
import functools

import jax
import jax.numpy as jnp
from jax import lax
from jax.experimental import pallas as pl
from jax.experimental.pallas import tpu as pltpu
from jax.sharding import PartitionSpec as P

PAIRS = 9
SITES = 8
FLAT = PAIRS * SITES
BOND = 8
LANES = 128
STEP = 1024
WRITES = 4
MESH = pl.DeviceIdType.MESH
HIGHEST = lax.Precision.HIGHEST
F32 = jnp.float32
BF16 = jnp.bfloat16


def iota(shape, dim):
    return lax.broadcasted_iota(jnp.int32, shape, dim)


def dot32(a, b):
    return jnp.dot(a, b, precision=HIGHEST, preferred_element_type=F32)


def dot16(a, b):
    return jnp.dot(a, b, preferred_element_type=F32)


def sign_tile(par):
    shape = (FLAT, 128)
    pair = iota(shape, 0) // SITES
    lane = iota(shape, 1) % (BOND * BOND)
    ket, bra = lane // BOND, lane % BOND
    par_ket = jnp.zeros(shape, jnp.int32)
    par_bra = jnp.zeros(shape, jnp.int32)
    for bond in range(BOND):
        value = par[bond]
        par_ket = jnp.where(ket == bond, value, par_ket)
        par_bra = jnp.where(bra == bond, value, par_bra)
    exponent = jnp.minimum(pair // 3, 1) * par_ket + jnp.minimum(pair % 3, 1) * par_bra
    return (1 - 2 * (exponent % 2)).astype(F32)


def compact(grams, shifts):
    square = (FLAT, FLAT)
    row_site, col_site = iota(square, 0) % SITES, iota(square, 1) % SITES
    rows = jnp.concatenate(
        [jnp.where(col_site == row_site + shift, gram, 0.0) for gram, shift in zip(grams, shifts, strict=True)],
        axis=0,
    )
    spread = (FLAT, LANES)
    source, lane = iota(spread, 0), iota(spread, 1)
    wide = dot32(rows, (lane % PAIRS == source // SITES).astype(F32))
    keep = lane // PAIRS == source // SITES
    out = []
    for i in range(len(grams)):
        part = jnp.where(keep, wide[i * FLAT : (i + 1) * FLAT], 0.0)
        out.append(part.reshape(PAIRS, SITES, LANES).sum(axis=0))
    return out


def rolled(rows, shift):
    shift %= SITES
    if not shift:
        return rows
    return jnp.concatenate([rows[shift:], rows[:shift]], axis=0)


def lane_coupling(ham):
    shape = (PAIRS, PAIRS)
    p, q = iota(shape, 0), iota(shape, 1)

    def charge(state):
        return jnp.minimum(state, 1)

    same = charge(p // 3) + charge(q // 3) == charge(p % 3) + charge(q % 3)
    coupling = jnp.where(same, ham, 0.0)
    shape = (PAIRS, LANES)
    row, lane = iota(shape, 0), iota(shape, 1)
    wide = dot32(coupling, (lane % PAIRS == row).astype(F32))
    return jnp.where(lane // PAIRS == row, wide, 0.0).sum(axis=0, keepdims=True)


def finish(density, coupling, factor):
    entries = PAIRS * PAIRS
    norm = jnp.sqrt((density * density).sum(axis=1, keepdims=True) / entries + 1e-06)
    trace = (coupling * density).sum(axis=1, keepdims=True)
    energy = factor * trace / norm
    lam = factor * (coupling / norm - trace / (entries * norm**3) * density)
    return energy, lam.astype(BF16).astype(F32)


def block(rows, shift, transposed, exact):
    shape = (FLAT, LANES)
    row, lane = iota(shape, 0), iota(shape, 1)
    tall = jnp.concatenate([rolled(rows, -shift) if transposed else rows] * PAIRS, axis=0)
    mine = lane % PAIRS if transposed else lane // PAIRS
    tall = jnp.where(mine == row // SITES, tall, 0.0)
    shape = (LANES, FLAT)
    source, col = iota(shape, 0), iota(shape, 1)
    other = source // PAIRS if transposed else source % PAIRS
    pick = (other == col // SITES).astype(F32)
    wide = dot32(tall, pick) if exact else dot16(tall.astype(BF16), pick.astype(BF16))
    shape = (FLAT, FLAT)
    row_site, col_site = iota(shape, 0) % SITES, iota(shape, 1) % SITES
    hit = row_site == col_site + shift if transposed else col_site == row_site + shift
    return jnp.where(hit, wide, 0.0)


def thirds(value):
    high = value.astype(BF16)
    rest = value - high.astype(F32)
    middle = rest.astype(BF16)
    return high, middle, (rest - middle.astype(F32)).astype(BF16)


def kernel(
    nx, ny, rows_total,
    right, left, down, up, ham_hbm, par_hbm,
    g_right, g_left, g_down, g_up, totals,
    v_right, v_left, v_down, v_up, from_above, from_below, ham, par, sign,
    gram_h, gram_dd, gram_uu, gram_d, gram_u, early_x, early_y, early_z, late_xy, late_z,
    late_above, late_below, buf_row,
    load_sem, down_send, down_recv, up_send, up_recv,
    ex_send, ex_recv, ey_send, ey_recv, ez_send, ez_recv,
    xy_send, xy_recv, z_send, z_recv,
    above_send, above_recv, below_send, below_recv, row_send, row_recv, relay,
):
    cut = right.shape[2]
    half = cut // 2
    steps = half // STEP
    row, col = lax.axis_index("row"), lax.axis_index("col")
    x, y, hi = col % nx, col // nx % ny, col // (nx * ny)
    plane = nx * ny
    here = y * nx + x
    has_above, has_below = row > 0, row < rows_total - 1

    pairs = (
        (ham_hbm, ham), (par_hbm, par), (right, v_right), (left, v_left), (down, v_down), (up, v_up),
    )
    loads = [
        pltpu.make_async_copy(source, target, load_sem.at[i]) for i, (source, target) in enumerate(pairs)
    ]
    for load in loads:
        load.start()

    core, depth = row % 2, rows_total // 2
    z_count = 2 * depth
    z = hi * depth + row // 2

    def device(dx=0, dy=0, dz=0, other=False):
        at_z = (z + dz) % z_count
        place = (y + dy) % ny * nx + (x + dx) % nx
        return (at_z % depth * 2 + (1 - core if other else core), at_z // depth * plane + place)

    def signal(semaphore, target):
        pl.semaphore_signal(semaphore, inc=1, device_id=target, device_id_type=MESH)

    barrier = pltpu.get_barrier_semaphore()
    near = [device(dx=1), device(dx=-1), device(dy=1), device(dy=-1), device(other=True)]
    near += [device(dz=step, other=other) for step in (1, -1) for other in (False, True)]
    for target in near:
        signal(barrier, target)
    pl.semaphore_wait(barrier, len(near))
    for i, target in enumerate((device(dx=-1), device(dy=-1), device(dz=1), device(dz=-1))):
        signal(relay.at[i], target)

    def span(start):
        return pl.ds(pl.multiple_of(start, STEP), STEP)

    def send_down(i):
        at = span(i * STEP)
        return pltpu.make_async_remote_copy(
            down.at[:, :, at], from_above.at[:, :, at], down_send.at[i], down_recv.at[i],
            device_id=(row + 1, col), device_id_type=MESH,
        )

    def up_start(i):
        return (i * STEP + half) % cut

    def send_up(i):
        at = span(up_start(i))
        return pltpu.make_async_remote_copy(
            up.at[:, :, at], from_below.at[:, :, at], up_send.at[i], up_recv.at[i],
            device_id=(row - 1, col), device_id_type=MESH,
        )

    for i in range(steps):

        @pl.when(has_below)
        def _(i=i):
            send_down(i).start()

        @pl.when(has_above)
        def _(i=i):
            send_up(i).start()

    for load in loads[:2]:
        load.wait()
    tile = sign_tile(par).astype(BF16)
    sign[...] = jnp.concatenate([tile] * (STEP // 128), axis=1)
    coupling = lane_coupling(ham[...])

    def flat(ref, at):
        return ref[:, :, at].reshape(FLAT, STEP)

    def signed(ref, at):
        value = flat(ref, at) * sign[...]
        ref[:, :, at] = value.reshape(PAIRS, SITES, STEP)
        return value

    def product(first, second):
        return lax.dot_general(first, second, (((1,), (1,)), ((), ())), preferred_element_type=F32)

    for gram in (gram_h, gram_dd, gram_uu, gram_d, gram_u):
        gram[...] = jnp.zeros_like(gram)
    for load in loads[2:]:
        load.wait()

    @pl.loop(0, 2 * steps)
    def _(i):
        at = span(i * STEP)
        data = jnp.concatenate([flat(v_right, at), signed(v_left, at)], axis=0)
        gram_h[...] += product(data, data)
        data = flat(v_down, at)
        gram_dd[...] += product(data, data)
        data = signed(v_up, at)
        gram_uu[...] += product(data, data)

    def gather(value, buf, me, devices, send, recv):
        buf[me] = value
        copies = [
            pltpu.make_async_remote_copy(
                buf.at[me], buf.at[me], send.at[i], recv.at[me], device_id=device, device_id_type=MESH
            )
            for i, device in enumerate(devices)
        ]
        for copy in copies:
            copy.start()
        return copies

    def arrived(buf, slot, recv):
        pltpu.make_async_remote_copy(
            buf.at[slot], buf.at[slot], recv.at[slot], recv.at[slot], device_id=(row, col), device_id_type=MESH
        ).wait_recv()

    def all_arrived(buf, me, recv):
        count = buf.shape[0]
        for i in range(1, count):
            arrived(buf, (me + i) % count, recv)
        value = buf[0]
        for i in range(1, count):
            value = value + buf[i]
        return value

    early = compact(
        [gram_h[:FLAT, FLAT:], gram_h[:FLAT, :FLAT], gram_h[FLAT:, FLAT:], gram_dd[...], gram_uu[...]],
        [1, 0, 0, 0, 0],
    )
    early[2] = rolled(early[2], 1)
    for i in range(4):
        pl.semaphore_wait(relay.at[i], 1)
    for i, step in enumerate((2, -2)):
        signal(relay.at[4 + i], device(dz=step))
    same_x = [device(dx=i) for i in range(1, nx)]
    same_y = [device(dy=i) for i in range(1, ny)]
    same_plane = [device(dx=i % nx, dy=i // nx) for i in range(1, plane)]
    sends = gather(jnp.concatenate(early, axis=1), early_x, x, same_x, ex_send, ex_recv)

    def meet(i):
        at, at_up = span(i * STEP), span(up_start(i))

        @pl.when(has_above)
        def _():
            send_down(i).wait_recv()
            gram_u[...] += product(flat(from_above, at), flat(v_up, at))

        @pl.when(has_below)
        def _():
            send_up(i).wait_recv()
            gram_d[...] += product(flat(v_down, at_up), signed(from_below, at_up))
            send_down(i).wait_send()
            send_down(i + steps).start()

        @pl.when(has_above)
        def _():
            send_up(i).wait_send()
            send_up(i + steps).start()

    for i in range(steps // 2):
        meet(i)
    early = all_arrived(early_x, x, ex_recv)
    sends += gather(early, early_y, y, same_y, ey_send, ey_recv)
    for i in range(steps // 2, steps):
        meet(i)

    late = jnp.concatenate(compact([gram_d[...], gram_u[...]], [0, 0]), axis=1)
    early = all_arrived(early_y, y, ey_recv)
    sends += gather(late, late_xy, here, same_plane, xy_send, xy_recv)
    for i in (4, 5):
        pl.semaphore_wait(relay.at[i], 1)
    partner = device(dz=depth)
    sends += gather(early, early_z, hi, [partner], ez_send, ez_recv)
    late = all_arrived(late_xy, here, xy_recv)

    sends += gather(late, late_z, hi, [partner], z_send, z_recv)

    def to_below(z):
        return pltpu.make_async_remote_copy(
            late_z.at[hi, :, pl.ds(0, LANES)], late_above.at[hi],
            below_send.at[z], above_recv.at[hi], device_id=(row + 1, z * plane + here), device_id_type=MESH,
        )

    def to_above(z):
        return pltpu.make_async_remote_copy(
            late_z.at[hi, :, pl.ds(LANES, LANES)], late_below.at[hi],
            above_send.at[z], below_recv.at[hi], device_id=(row - 1, z * plane + here), device_id_type=MESH,
        )

    @pl.when(has_below)
    def _():
        for z in (0, 1):
            to_below(z).start()

    @pl.when(has_above)
    def _():
        for z in (0, 1):
            to_above(z).start()

    early = all_arrived(early_z, hi, ez_recv)
    density_h, rr, ll, dd, uu = [early[:, i * LANES : (i + 1) * LANES] for i in range(5)]
    rr, ll, dd, uu = [thirds(block(g, 0, False, True)) for g in (rr, ll, dd, uu)]
    site = iota((SITES, 1), 0).astype(F32)
    weight = 1.0 + 2.0 * site / SITES + row.astype(F32) / rows_total
    weight_above = 1.0 + 2.0 * site / SITES + (row - 1).astype(F32) / rows_total
    energy_h, lam_h = finish(density_h, coupling, jnp.where(site < SITES - 1, weight, 0.0))
    weights = block(lam_h, 0, False, False)
    small = weights.astype(BF16)
    total_h = sum(dot16(small, g) for g in ll) + sum(dot16(g, small) for g in rr)
    square_h = (total_h * weights).sum()
    to_right = block(lam_h, 1, False, False).astype(BF16)
    to_left = block(lam_h, 1, True, False).astype(BF16)

    def put(ref, at, value):
        ref[:, :, at] = value.reshape(PAIRS, SITES, STEP)

    @pl.loop(0, 2 * steps)
    def _(i):
        at = span(i * STEP)
        put(g_right, at, dot16(to_right, flat(v_left, at)))
        put(g_left, at, dot16(to_left, flat(v_right, at)) * sign[...].astype(F32))

    late = all_arrived(late_z, hi, z_recv)

    @pl.when(has_above)
    def _():
        for z in (0, 1):
            arrived(late_above, z, above_recv)

    @pl.when(has_below)
    def _():
        for z in (0, 1):
            arrived(late_below, z, below_recv)

    @pl.when(jnp.logical_not(has_above))
    def _():
        late_above[...] = jnp.zeros_like(late_above)

    @pl.when(jnp.logical_not(has_below))
    def _():
        late_below[...] = jnp.zeros_like(late_below)

    density_v = late[:, :LANES] + (late_below[0] + late_below[1])
    density_w = (late_above[0] + late_above[1]) + late[:, LANES:]
    energy_v, lam_v = finish(density_v, coupling, weight * has_below.astype(F32))
    _, lam_w = finish(density_w, coupling, weight_above * has_above.astype(F32))
    weights_v, weights_w = block(lam_v, 0, False, False), block(lam_w, 0, False, False)
    to_down, small = weights_v.astype(BF16), weights_w.astype(BF16)
    total_v = sum(dot16(g, to_down) for g in dd)
    total_w = sum(dot16(small, g) for g in uu)
    square = square_h + (total_v * weights_v + total_w * weights_w).sum()
    energies = (energy_h + energy_v).sum()
    lane = iota((SITES, LANES), 1)
    message = jnp.where(lane == 0, square, jnp.where(lane == 1, energies, 0.0))
    mates = [device(dz=step, other=other) for step in (0, 1, -1, 2) for other in (False, True)][1:]
    sends += gather(message, buf_row, row, mates, row_send, row_recv)
    to_up = block(lam_w, 0, True, False).astype(BF16)

    @pl.loop(0, 2 * steps)
    def _(i):
        at, at_up = span(i * STEP), span(up_start(i))

        @pl.when(has_above)
        def _():
            @pl.when(i >= steps)
            def _():
                send_down(i).wait_recv()

            put(g_up, at, dot16(to_up, flat(from_above, at)) * sign[...].astype(F32))

        @pl.when(has_below)
        def _():
            @pl.when(i >= steps)
            def _():
                send_up(i).wait_recv()
                signed(from_below, at_up)

            put(g_down, at_up, dot16(to_down, flat(from_below, at_up)))

    @pl.when(jnp.logical_not(has_above))
    def _():
        g_up[...] = jnp.zeros_like(g_up)

    @pl.when(jnp.logical_not(has_below))
    def _():
        g_down[...] = jnp.zeros_like(g_down)

    @pl.when(has_below)
    def _():
        for i in range(steps, 2 * steps):
            send_down(i).wait_send()
        for z in (0, 1):
            to_below(z).wait_send()

    @pl.when(has_above)
    def _():
        for i in range(steps, 2 * steps):
            send_up(i).wait_send()
        for z in (0, 1):
            to_above(z).wait_send()

    totals[...] = all_arrived(buf_row, row, row_recv)
    for copy in sends:
        copy.wait_send()


def scale_kernel(
    count, totals, raw_right, raw_left, raw_down, raw_up,
    g_right, g_left, g_down, g_up, energy, o_right, o_left, o_down, o_up, o_energy, sems, energy_sem,
):
    message = totals[...]
    square = jnp.maximum(message[:1, :1], 0.0)
    scale = 1.0 / jnp.sqrt(square / count + 1e-06)
    o_energy[...] = message[:1, 1:2] / SITES
    copies = [pltpu.make_async_copy(o_energy, energy, energy_sem)]
    copies[0].start()
    cut = raw_right.shape[2]
    width = cut // WRITES
    arrays = (
        (raw_right, o_right, g_right), (raw_left, o_left, g_left), (raw_down, o_down, g_down), (raw_up, o_up, g_up),
    )
    for a, (raw, out, target) in enumerate(arrays):
        for i in range(WRITES):
            at = pl.ds(i * width, width)

            @pl.loop(0, PAIRS)
            def _(p, raw=raw, out=out, at=at):
                out[p, :, at] = (raw[p, :, at] * scale).astype(BF16)

            copies.append(pltpu.make_async_copy(out.at[:, :, at], target.at[:, :, at], sems.at[a, i]))
            copies[-1].start()
    for copy in copies:
        copy.wait()


def shards(nx, ny, cols_total, right_env, left_env, down_env, up_env, hamiltonian, parity):
    rows_total = lax.axis_size("row")
    cut = right_env.shape[3]
    chunks = cut // STEP
    envs = [e.transpose(0, 2, 1, 3).reshape(PAIRS, SITES, cut) for e in (right_env, left_env, down_env, up_env)]
    env = (PAIRS, SITES, cut)
    dma = pltpu.SemaphoreType.DMA
    hbm_spec = pl.BlockSpec(memory_space=pltpu.HBM)
    vmem_spec = pl.BlockSpec(memory_space=pltpu.VMEM)
    square = pltpu.VMEM((FLAT, FLAT), F32)
    early, late = 5 * LANES, 2 * LANES
    raw = pl.pallas_call(
        functools.partial(kernel, nx, ny, rows_total),
        out_shape=[pltpu.VMEM(env, F32)] * 4 + [pltpu.VMEM((SITES, LANES), F32)],
        in_specs=[hbm_spec] * 6,
        out_specs=[vmem_spec] * 5,
        scratch_shapes=[pltpu.VMEM(env, BF16)] * 6
        + [
            pltpu.VMEM((PAIRS, PAIRS), F32),
            pltpu.SMEM((BOND,), jnp.int32),
            pltpu.VMEM((FLAT, STEP), BF16),
            pltpu.VMEM((2 * FLAT, 2 * FLAT), F32),
            square, square, square, square,
            pltpu.VMEM((nx, SITES, early), F32),
            pltpu.VMEM((ny, SITES, early), F32),
            pltpu.VMEM((2, SITES, early), F32),
            pltpu.VMEM((nx * ny, SITES, late), F32),
            pltpu.VMEM((2, SITES, late), F32),
            pltpu.VMEM((2, SITES, LANES), F32),
            pltpu.VMEM((2, SITES, LANES), F32),
            pltpu.VMEM((rows_total, SITES, LANES), F32),
            dma((6,)),
            dma((chunks,)), dma((chunks,)), dma((chunks,)), dma((chunks,)),
            dma((nx,)), dma((nx,)), dma((ny,)), dma((ny,)), dma((2,)), dma((2,)),
            dma((nx * ny,)), dma((nx * ny,)), dma((2,)), dma((2,)),
            dma((2,)), dma((2,)), dma((2,)), dma((2,)), dma((rows_total,)), dma((rows_total,)),
            pltpu.SemaphoreType.REGULAR((6,)),
        ],
        compiler_params=pltpu.CompilerParams(
            collective_id=0, has_side_effects=True, vmem_limit_bytes=32 * 1024 * 1024
        ),
    )(*[pltpu.with_memory_space_constraint(a, pltpu.HBM) for a in (*envs, hamiltonian, parity)])
    count = 4.0 * rows_total * FLAT * cols_total * cut
    outs = pl.pallas_call(
        functools.partial(scale_kernel, count),
        out_shape=[jax.ShapeDtypeStruct(env, BF16)] * 4 + [jax.ShapeDtypeStruct((1, 1), F32)],
        in_specs=[vmem_spec] * 5,
        out_specs=[hbm_spec] * 5,
        scratch_shapes=[pltpu.VMEM(env, BF16)] * 4 + [pltpu.VMEM((1, 1), F32), dma((4, WRITES)), dma],
        compiler_params=pltpu.CompilerParams(vmem_limit_bytes=16 * 1024 * 1024),
    )(*[pltpu.with_memory_space_constraint(a, pltpu.VMEM) for a in (raw[4], *raw[:4])])
    grads = [g.reshape(1, PAIRS, SITES, cut).transpose(0, 2, 1, 3) for g in outs[:4]]
    return (*grads, outs[4].reshape(()))


def solution(mesh):
    spec = P("row", None, None, "col")
    side = 4
    return jax.shard_map(
        functools.partial(shards, side, mesh.shape["col"] // (2 * side), mesh.shape["col"]),
        mesh=mesh,
        in_specs=(spec, spec, spec, spec, P(), P()),
        out_specs=(spec, spec, spec, spec, P()),
        check_vma=False,
    )
```

```python
import functools

import jax
import jax.numpy as jnp
from jax import lax
from jax.experimental import pallas as pl
from jax.experimental.pallas import tpu as pltpu
from jax.sharding import PartitionSpec as P

PAIRS = 9
SITES = 8
FLAT = PAIRS * SITES
BOND = 8
LANES = 128
STEP = 1024
MESH = pl.DeviceIdType.MESH
HIGHEST = lax.Precision.HIGHEST
F32 = jnp.float32
BF16 = jnp.bfloat16


def iota(shape, dim):
    return lax.broadcasted_iota(jnp.int32, shape, dim)


def dot32(a, b):
    return jnp.dot(a, b, precision=HIGHEST, preferred_element_type=F32)


def dot16(a, b):
    return jnp.dot(a, b, preferred_element_type=F32)


def sign_tile(par):
    shape = (FLAT, 128)
    pair = iota(shape, 0) // SITES
    lane = iota(shape, 1) % (BOND * BOND)
    ket, bra = lane // BOND, lane % BOND
    par_ket = jnp.zeros(shape, jnp.int32)
    par_bra = jnp.zeros(shape, jnp.int32)
    for bond in range(BOND):
        value = par[bond]
        par_ket = jnp.where(ket == bond, value, par_ket)
        par_bra = jnp.where(bra == bond, value, par_bra)
    exponent = jnp.minimum(pair // 3, 1) * par_ket + jnp.minimum(pair % 3, 1) * par_bra
    return (1 - 2 * (exponent % 2)).astype(F32)


def compact(grams, shifts):
    square = (FLAT, FLAT)
    row_site, col_site = iota(square, 0) % SITES, iota(square, 1) % SITES
    rows = jnp.concatenate(
        [jnp.where(col_site == row_site + shift, gram, 0.0) for gram, shift in zip(grams, shifts, strict=True)],
        axis=0,
    )
    spread = (FLAT, LANES)
    source, lane = iota(spread, 0), iota(spread, 1)
    wide = dot32(rows, (lane % PAIRS == source // SITES).astype(F32))
    keep = lane // PAIRS == source // SITES
    out = []
    for i in range(len(grams)):
        part = jnp.where(keep, wide[i * FLAT : (i + 1) * FLAT], 0.0)
        out.append(part.reshape(PAIRS, SITES, LANES).sum(axis=0))
    return out


def rolled(rows, shift):
    shift %= SITES
    if not shift:
        return rows
    return jnp.concatenate([rows[shift:], rows[:shift]], axis=0)


def lane_coupling(ham):
    shape = (PAIRS, PAIRS)
    p, q = iota(shape, 0), iota(shape, 1)

    def charge(state):
        return jnp.minimum(state, 1)

    same = charge(p // 3) + charge(q // 3) == charge(p % 3) + charge(q % 3)
    coupling = jnp.where(same, ham, 0.0)
    shape = (PAIRS, LANES)
    row, lane = iota(shape, 0), iota(shape, 1)
    wide = dot32(coupling, (lane % PAIRS == row).astype(F32))
    return jnp.where(lane // PAIRS == row, wide, 0.0).sum(axis=0, keepdims=True)


def finish(density, coupling, factor):
    entries = PAIRS * PAIRS
    norm = jnp.sqrt((density * density).sum(axis=1, keepdims=True) / entries + 1e-06)
    trace = (coupling * density).sum(axis=1, keepdims=True)
    energy = factor * trace / norm
    lam = factor * (coupling / norm - trace / (entries * norm**3) * density)
    return energy, lam.astype(BF16).astype(F32)


def block(rows, shift, transposed, exact):
    shape = (FLAT, LANES)
    row, lane = iota(shape, 0), iota(shape, 1)
    tall = jnp.concatenate([rolled(rows, -shift) if transposed else rows] * PAIRS, axis=0)
    mine = lane % PAIRS if transposed else lane // PAIRS
    tall = jnp.where(mine == row // SITES, tall, 0.0)
    shape = (LANES, FLAT)
    source, col = iota(shape, 0), iota(shape, 1)
    other = source // PAIRS if transposed else source % PAIRS
    pick = (other == col // SITES).astype(F32)
    wide = dot32(tall, pick) if exact else dot16(tall.astype(BF16), pick.astype(BF16))
    shape = (FLAT, FLAT)
    row_site, col_site = iota(shape, 0) % SITES, iota(shape, 1) % SITES
    hit = row_site == col_site + shift if transposed else col_site == row_site + shift
    return jnp.where(hit, wide, 0.0)


def thirds(value):
    high = value.astype(BF16)
    rest = value - high.astype(F32)
    middle = rest.astype(BF16)
    return high, middle, (rest - middle.astype(F32)).astype(BF16)


def kernel(
    nx, ny, rows_total,
    right, left, down, up, ham_hbm, par_hbm,
    g_right, g_left, g_down, g_up, totals,
    v_right, v_left, v_down, v_up, from_above, from_below, ham, par, sign,
    gram_h, gram_dd, gram_uu, gram_d, gram_u, early_x, early_y, early_z, late_xy, late_z,
    late_above, late_below, buf_row,
    load_sem, down_send, down_recv, up_send, up_recv,
    ex_send, ex_recv, ey_send, ey_recv, ez_send, ez_recv,
    xy_send, xy_recv, z_send, z_recv,
    above_send, above_recv, below_send, below_recv, row_send, row_recv, relay,
):
    cut = right.shape[2]
    half = cut // 2
    steps = half // STEP
    row, col = lax.axis_index("row"), lax.axis_index("col")
    x, y, hi = col % nx, col // nx % ny, col // (nx * ny)
    plane = nx * ny
    here = y * nx + x
    has_above, has_below = row > 0, row < rows_total - 1

    pairs = (
        (ham_hbm, ham), (par_hbm, par), (right, v_right), (left, v_left), (down, v_down), (up, v_up),
    )
    loads = [
        pltpu.make_async_copy(source, target, load_sem.at[i]) for i, (source, target) in enumerate(pairs)
    ]
    for load in loads:
        load.start()

    core, depth = row % 2, rows_total // 2
    z_count = 2 * depth
    z = hi * depth + row // 2

    def device(dx=0, dy=0, dz=0, other=False):
        at_z = (z + dz) % z_count
        place = (y + dy) % ny * nx + (x + dx) % nx
        return (at_z % depth * 2 + (1 - core if other else core), at_z // depth * plane + place)

    def signal(semaphore, target):
        pl.semaphore_signal(semaphore, inc=1, device_id=target, device_id_type=MESH)

    barrier = pltpu.get_barrier_semaphore()
    near = [device(dx=1), device(dx=-1), device(dy=1), device(dy=-1), device(other=True)]
    near += [device(dz=step, other=other) for step in (1, -1) for other in (False, True)]
    for target in near:
        signal(barrier, target)
    pl.semaphore_wait(barrier, len(near))
    for i, target in enumerate((device(dx=-1), device(dy=-1), device(dz=1), device(dz=-1))):
        signal(relay.at[i], target)

    def span(start):
        return pl.ds(pl.multiple_of(start, STEP), STEP)

    def send_down(i):
        at = span(i * STEP)
        return pltpu.make_async_remote_copy(
            down.at[:, :, at], from_above.at[:, :, at], down_send.at[i], down_recv.at[i],
            device_id=(row + 1, col), device_id_type=MESH,
        )

    def up_start(i):
        return (i * STEP + half) % cut

    def send_up(i):
        at = span(up_start(i))
        return pltpu.make_async_remote_copy(
            up.at[:, :, at], from_below.at[:, :, at], up_send.at[i], up_recv.at[i],
            device_id=(row - 1, col), device_id_type=MESH,
        )

    for i in range(steps):

        @pl.when(has_below)
        def _(i=i):
            send_down(i).start()

        @pl.when(has_above)
        def _(i=i):
            send_up(i).start()

    for load in loads[:2]:
        load.wait()
    tile = sign_tile(par).astype(BF16)
    sign[...] = jnp.concatenate([tile] * (STEP // 128), axis=1)
    coupling = lane_coupling(ham[...])

    def flat(ref, at):
        return ref[:, :, at].reshape(FLAT, STEP)

    def signed(ref, at):
        value = flat(ref, at) * sign[...]
        ref[:, :, at] = value.reshape(PAIRS, SITES, STEP)
        return value

    def product(first, second):
        return lax.dot_general(first, second, (((1,), (1,)), ((), ())), preferred_element_type=F32)

    for gram in (gram_h, gram_dd, gram_uu, gram_d, gram_u):
        gram[...] = jnp.zeros_like(gram)
    for load in loads[2:]:
        load.wait()

    @pl.loop(0, 2 * steps)
    def _(i):
        at = span(i * STEP)
        data = jnp.concatenate([flat(v_right, at), signed(v_left, at)], axis=0)
        gram_h[...] += product(data, data)
        data = flat(v_down, at)
        gram_dd[...] += product(data, data)
        data = signed(v_up, at)
        gram_uu[...] += product(data, data)

    def gather(value, buf, me, devices, send, recv):
        buf[me] = value
        copies = [
            pltpu.make_async_remote_copy(
                buf.at[me], buf.at[me], send.at[i], recv.at[me], device_id=device, device_id_type=MESH
            )
            for i, device in enumerate(devices)
        ]
        for copy in copies:
            copy.start()
        return copies

    def arrived(buf, slot, recv):
        pltpu.make_async_remote_copy(
            buf.at[slot], buf.at[slot], recv.at[slot], recv.at[slot], device_id=(row, col), device_id_type=MESH
        ).wait_recv()

    def all_arrived(buf, me, recv):
        count = buf.shape[0]
        for i in range(1, count):
            arrived(buf, (me + i) % count, recv)
        value = buf[0]
        for i in range(1, count):
            value = value + buf[i]
        return value

    early = compact(
        [gram_h[:FLAT, FLAT:], gram_h[:FLAT, :FLAT], gram_h[FLAT:, FLAT:], gram_dd[...], gram_uu[...]],
        [1, 0, 0, 0, 0],
    )
    early[2] = rolled(early[2], 1)
    for i in range(4):
        pl.semaphore_wait(relay.at[i], 1)
    for i, step in enumerate((2, -2)):
        signal(relay.at[4 + i], device(dz=step))
    same_x = [device(dx=i) for i in range(1, nx)]
    same_y = [device(dy=i) for i in range(1, ny)]
    same_plane = [device(dx=i % nx, dy=i // nx) for i in range(1, plane)]
    sends = gather(jnp.concatenate(early, axis=1), early_x, x, same_x, ex_send, ex_recv)

    def meet(i):
        at, at_up = span(i * STEP), span(up_start(i))

        @pl.when(has_above)
        def _():
            send_down(i).wait_recv()
            gram_u[...] += product(flat(from_above, at), flat(v_up, at))

        @pl.when(has_below)
        def _():
            send_up(i).wait_recv()
            gram_d[...] += product(flat(v_down, at_up), signed(from_below, at_up))
            send_down(i).wait_send()
            send_down(i + steps).start()

        @pl.when(has_above)
        def _():
            send_up(i).wait_send()
            send_up(i + steps).start()

    for i in range(steps // 2):
        meet(i)
    early = all_arrived(early_x, x, ex_recv)
    sends += gather(early, early_y, y, same_y, ey_send, ey_recv)
    for i in range(steps // 2, steps):
        meet(i)

    late = jnp.concatenate(compact([gram_d[...], gram_u[...]], [0, 0]), axis=1)
    sends += gather(late, late_xy, here, same_plane, xy_send, xy_recv)
    early = all_arrived(early_y, y, ey_recv)
    for i in (4, 5):
        pl.semaphore_wait(relay.at[i], 1)
    partner = device(dz=depth)
    sends += gather(early, early_z, hi, [partner], ez_send, ez_recv)
    late = all_arrived(late_xy, here, xy_recv)

    sends += gather(late, late_z, hi, [partner], z_send, z_recv)

    def to_below(z):
        return pltpu.make_async_remote_copy(
            late_z.at[hi, :, pl.ds(0, LANES)], late_above.at[hi],
            below_send.at[z], above_recv.at[hi], device_id=(row + 1, z * plane + here), device_id_type=MESH,
        )

    def to_above(z):
        return pltpu.make_async_remote_copy(
            late_z.at[hi, :, pl.ds(LANES, LANES)], late_below.at[hi],
            above_send.at[z], below_recv.at[hi], device_id=(row - 1, z * plane + here), device_id_type=MESH,
        )

    @pl.when(has_below)
    def _():
        for z in (0, 1):
            to_below(z).start()

    @pl.when(has_above)
    def _():
        for z in (0, 1):
            to_above(z).start()

    early = all_arrived(early_z, hi, ez_recv)
    density_h, rr, ll, dd, uu = [early[:, i * LANES : (i + 1) * LANES] for i in range(5)]
    rr, ll, dd, uu = [thirds(block(g, 0, False, True)) for g in (rr, ll, dd, uu)]
    site = iota((SITES, 1), 0).astype(F32)
    weight = 1.0 + 2.0 * site / SITES + row.astype(F32) / rows_total
    weight_above = 1.0 + 2.0 * site / SITES + (row - 1).astype(F32) / rows_total
    energy_h, lam_h = finish(density_h, coupling, jnp.where(site < SITES - 1, weight, 0.0))
    weights = block(lam_h, 0, False, False)
    small = weights.astype(BF16)
    total_h = sum(dot16(small, g) for g in ll) + sum(dot16(g, small) for g in rr)
    square_h = (total_h * weights).sum()
    to_right = block(lam_h, 1, False, False).astype(BF16)
    to_left = block(lam_h, 1, True, False).astype(BF16)

    def put(ref, at, value):
        ref[:, :, at] = value.reshape(PAIRS, SITES, STEP)

    @pl.loop(0, 2 * steps)
    def _(i):
        at = span(i * STEP)
        put(g_right, at, dot16(to_right, flat(v_left, at)))
        put(g_left, at, dot16(to_left, flat(v_right, at)) * sign[...].astype(F32))

    late = all_arrived(late_z, hi, z_recv)

    @pl.when(has_above)
    def _():
        for z in (0, 1):
            arrived(late_above, z, above_recv)

    @pl.when(has_below)
    def _():
        for z in (0, 1):
            arrived(late_below, z, below_recv)

    @pl.when(jnp.logical_not(has_above))
    def _():
        late_above[...] = jnp.zeros_like(late_above)

    @pl.when(jnp.logical_not(has_below))
    def _():
        late_below[...] = jnp.zeros_like(late_below)

    density_v = late[:, :LANES] + (late_below[0] + late_below[1])
    density_w = (late_above[0] + late_above[1]) + late[:, LANES:]
    energy_v, lam_v = finish(density_v, coupling, weight * has_below.astype(F32))
    _, lam_w = finish(density_w, coupling, weight_above * has_above.astype(F32))
    weights_v, weights_w = block(lam_v, 0, False, False), block(lam_w, 0, False, False)
    to_down, small = weights_v.astype(BF16), weights_w.astype(BF16)
    total_v = sum(dot16(g, to_down) for g in dd)
    total_w = sum(dot16(small, g) for g in uu)
    square = square_h + (total_v * weights_v + total_w * weights_w).sum()
    energies = (energy_h + energy_v).sum()
    lane = iota((SITES, LANES), 1)
    message = jnp.where(lane == 0, square, jnp.where(lane == 1, energies, 0.0))
    mates = [device(dz=step, other=other) for step in (0, 1, -1, 2) for other in (False, True)][1:]
    sends += gather(message, buf_row, row, mates, row_send, row_recv)
    to_up = block(lam_w, 0, True, False).astype(BF16)

    @pl.loop(0, 2 * steps)
    def _(i):
        at, at_up = span(i * STEP), span(up_start(i))

        @pl.when(has_above)
        def _():
            @pl.when(i >= steps)
            def _():
                send_down(i).wait_recv()

            put(g_up, at, dot16(to_up, flat(from_above, at)) * sign[...].astype(F32))

        @pl.when(has_below)
        def _():
            @pl.when(i >= steps)
            def _():
                send_up(i).wait_recv()
                signed(from_below, at_up)

            put(g_down, at_up, dot16(to_down, flat(from_below, at_up)))

    @pl.when(jnp.logical_not(has_above))
    def _():
        g_up[...] = jnp.zeros_like(g_up)

    @pl.when(jnp.logical_not(has_below))
    def _():
        g_down[...] = jnp.zeros_like(g_down)

    @pl.when(has_below)
    def _():
        for i in range(steps, 2 * steps):
            send_down(i).wait_send()
        for z in (0, 1):
            to_below(z).wait_send()

    @pl.when(has_above)
    def _():
        for i in range(steps, 2 * steps):
            send_up(i).wait_send()
        for z in (0, 1):
            to_above(z).wait_send()

    totals[...] = all_arrived(buf_row, row, row_recv)
    for copy in sends:
        copy.wait_send()


def scale_kernel(
    count, totals, raw_right, raw_left, raw_down, raw_up,
    g_right, g_left, g_down, g_up, energy, o_right, o_left, o_down, o_up, o_energy, sems, energy_sem,
):
    message = totals[...]
    square = jnp.maximum(message[:1, :1], 0.0)
    scale = 1.0 / jnp.sqrt(square / count + 1e-06)
    o_energy[...] = message[:1, 1:2] / SITES
    copies = [pltpu.make_async_copy(o_energy, energy, energy_sem)]
    copies[0].start()
    arrays = (
        (raw_right, o_right, g_right), (raw_left, o_left, g_left), (raw_down, o_down, g_down), (raw_up, o_up, g_up),
    )
    for a, (raw, out, target) in enumerate(arrays):
        for p in range(PAIRS):

            @pl.loop(0, raw.shape[2] // STEP, unroll=True)
            def _(i, p=p, raw=raw, out=out):
                at = pl.ds(pl.multiple_of(i * STEP, STEP), STEP)
                out[p, :, at] = (raw[p, :, at] * scale).astype(BF16)

            copies.append(pltpu.make_async_copy(out.at[p], target.at[p], sems.at[a, p]))
            copies[-1].start()
    for copy in copies:
        copy.wait()


def shards(nx, ny, cols_total, right_env, left_env, down_env, up_env, hamiltonian, parity):
    rows_total = lax.axis_size("row")
    cut = right_env.shape[3]
    chunks = cut // STEP
    envs = [e.transpose(0, 2, 1, 3).reshape(PAIRS, SITES, cut) for e in (right_env, left_env, down_env, up_env)]
    env = (PAIRS, SITES, cut)
    dma = pltpu.SemaphoreType.DMA
    hbm_spec = pl.BlockSpec(memory_space=pltpu.HBM)
    vmem_spec = pl.BlockSpec(memory_space=pltpu.VMEM)
    square = pltpu.VMEM((FLAT, FLAT), F32)
    early, late = 5 * LANES, 2 * LANES
    raw = pl.pallas_call(
        functools.partial(kernel, nx, ny, rows_total),
        out_shape=[pltpu.VMEM(env, F32)] * 4 + [pltpu.VMEM((SITES, LANES), F32)],
        in_specs=[hbm_spec] * 6,
        out_specs=[vmem_spec] * 5,
        scratch_shapes=[pltpu.VMEM(env, BF16)] * 6
        + [
            pltpu.VMEM((PAIRS, PAIRS), F32),
            pltpu.SMEM((BOND,), jnp.int32),
            pltpu.VMEM((FLAT, STEP), BF16),
            pltpu.VMEM((2 * FLAT, 2 * FLAT), F32),
            square, square, square, square,
            pltpu.VMEM((nx, SITES, early), F32),
            pltpu.VMEM((ny, SITES, early), F32),
            pltpu.VMEM((2, SITES, early), F32),
            pltpu.VMEM((nx * ny, SITES, late), F32),
            pltpu.VMEM((2, SITES, late), F32),
            pltpu.VMEM((2, SITES, LANES), F32),
            pltpu.VMEM((2, SITES, LANES), F32),
            pltpu.VMEM((rows_total, SITES, LANES), F32),
            dma((6,)),
            dma((chunks,)), dma((chunks,)), dma((chunks,)), dma((chunks,)),
            dma((nx,)), dma((nx,)), dma((ny,)), dma((ny,)), dma((2,)), dma((2,)),
            dma((nx * ny,)), dma((nx * ny,)), dma((2,)), dma((2,)),
            dma((2,)), dma((2,)), dma((2,)), dma((2,)), dma((rows_total,)), dma((rows_total,)),
            pltpu.SemaphoreType.REGULAR((6,)),
        ],
        compiler_params=pltpu.CompilerParams(
            collective_id=0, has_side_effects=True, vmem_limit_bytes=32 * 1024 * 1024
        ),
    )(*[pltpu.with_memory_space_constraint(a, pltpu.HBM) for a in (*envs, hamiltonian, parity)])
    count = 4.0 * rows_total * FLAT * cols_total * cut
    outs = pl.pallas_call(
        functools.partial(scale_kernel, count),
        out_shape=[jax.ShapeDtypeStruct(env, BF16)] * 4 + [jax.ShapeDtypeStruct((1, 1), F32)],
        in_specs=[vmem_spec] * 5,
        out_specs=[hbm_spec] * 5,
        scratch_shapes=[pltpu.VMEM(env, BF16)] * 4 + [pltpu.VMEM((1, 1), F32), dma((4, PAIRS)), dma],
        compiler_params=pltpu.CompilerParams(vmem_limit_bytes=16 * 1024 * 1024),
    )(*[pltpu.with_memory_space_constraint(a, pltpu.VMEM) for a in (raw[4], *raw[:4])])
    grads = [g.reshape(1, PAIRS, SITES, cut).transpose(0, 2, 1, 3) for g in outs[:4]]
    return (*grads, outs[4].reshape(()))


def solution(mesh):
    spec = P("row", None, None, "col")
    side = 4
    return jax.shard_map(
        functools.partial(shards, side, mesh.shape["col"] // (2 * side), mesh.shape["col"]),
        mesh=mesh,
        in_specs=(spec, spec, spec, spec, P(), P()),
        out_specs=(spec, spec, spec, spec, P()),
        check_vma=False,
    )
```

```python
import functools

import jax
import jax.numpy as jnp
from jax import lax
from jax.experimental import pallas as pl
from jax.experimental.pallas import tpu as pltpu
from jax.sharding import PartitionSpec as P

PAIRS = 9
SITES = 8
FLAT = PAIRS * SITES
BOND = 8
LANES = 128
STEP = 2048
MESH = pl.DeviceIdType.MESH
HIGHEST = lax.Precision.HIGHEST
F32 = jnp.float32
BF16 = jnp.bfloat16


def iota(shape, dim):
    return lax.broadcasted_iota(jnp.int32, shape, dim)


def dot32(a, b):
    return jnp.dot(a, b, precision=HIGHEST, preferred_element_type=F32)


def dot16(a, b):
    return jnp.dot(a, b, preferred_element_type=F32)


def sign_tile(par):
    shape = (FLAT, 128)
    pair = iota(shape, 0) // SITES
    lane = iota(shape, 1) % (BOND * BOND)
    ket, bra = lane // BOND, lane % BOND
    par_ket = jnp.zeros(shape, jnp.int32)
    par_bra = jnp.zeros(shape, jnp.int32)
    for bond in range(BOND):
        value = par[bond]
        par_ket = jnp.where(ket == bond, value, par_ket)
        par_bra = jnp.where(bra == bond, value, par_bra)
    exponent = jnp.minimum(pair // 3, 1) * par_ket + jnp.minimum(pair % 3, 1) * par_bra
    return (1 - 2 * (exponent % 2)).astype(F32)


def compact(grams, shifts):
    square = (FLAT, FLAT)
    row_site, col_site = iota(square, 0) % SITES, iota(square, 1) % SITES
    rows = jnp.concatenate(
        [jnp.where(col_site == row_site + shift, gram, 0.0) for gram, shift in zip(grams, shifts, strict=True)],
        axis=0,
    )
    spread = (FLAT, LANES)
    source, lane = iota(spread, 0), iota(spread, 1)
    wide = dot32(rows, (lane % PAIRS == source // SITES).astype(F32))
    keep = lane // PAIRS == source // SITES
    out = []
    for i in range(len(grams)):
        part = jnp.where(keep, wide[i * FLAT : (i + 1) * FLAT], 0.0)
        out.append(part.reshape(PAIRS, SITES, LANES).sum(axis=0))
    return out


def rolled(rows, shift):
    shift %= SITES
    if not shift:
        return rows
    return jnp.concatenate([rows[shift:], rows[:shift]], axis=0)


def lane_coupling(ham):
    shape = (PAIRS, PAIRS)
    p, q = iota(shape, 0), iota(shape, 1)

    def charge(state):
        return jnp.minimum(state, 1)

    same = charge(p // 3) + charge(q // 3) == charge(p % 3) + charge(q % 3)
    coupling = jnp.where(same, ham, 0.0)
    shape = (PAIRS, LANES)
    row, lane = iota(shape, 0), iota(shape, 1)
    wide = dot32(coupling, (lane % PAIRS == row).astype(F32))
    return jnp.where(lane // PAIRS == row, wide, 0.0).sum(axis=0, keepdims=True)


def finish(density, coupling, factor):
    entries = PAIRS * PAIRS
    norm = jnp.sqrt((density * density).sum(axis=1, keepdims=True) / entries + 1e-06)
    trace = (coupling * density).sum(axis=1, keepdims=True)
    energy = factor * trace / norm
    lam = factor * (coupling / norm - trace / (entries * norm**3) * density)
    return energy, lam.astype(BF16).astype(F32)


def block(rows, shift, transposed, exact):
    shape = (FLAT, LANES)
    row, lane = iota(shape, 0), iota(shape, 1)
    tall = jnp.concatenate([rolled(rows, -shift) if transposed else rows] * PAIRS, axis=0)
    mine = lane % PAIRS if transposed else lane // PAIRS
    tall = jnp.where(mine == row // SITES, tall, 0.0)
    shape = (LANES, FLAT)
    source, col = iota(shape, 0), iota(shape, 1)
    other = source // PAIRS if transposed else source % PAIRS
    pick = (other == col // SITES).astype(F32)
    wide = dot32(tall, pick) if exact else dot16(tall.astype(BF16), pick.astype(BF16))
    shape = (FLAT, FLAT)
    row_site, col_site = iota(shape, 0) % SITES, iota(shape, 1) % SITES
    hit = row_site == col_site + shift if transposed else col_site == row_site + shift
    return jnp.where(hit, wide, 0.0)


def thirds(value):
    high = value.astype(BF16)
    rest = value - high.astype(F32)
    middle = rest.astype(BF16)
    return high, middle, (rest - middle.astype(F32)).astype(BF16)


def kernel(
    nx, ny, rows_total,
    right, left, down, up, ham_hbm, par_hbm,
    g_right, g_left, g_down, g_up, totals,
    v_right, v_left, v_down, v_up, from_above, from_below, ham, par, sign,
    gram_h, gram_dd, gram_uu, gram_d, gram_u, early_x, early_y, early_z, late_xy, late_z,
    late_above, late_below, buf_row,
    load_sem, down_send, down_recv, up_send, up_recv,
    ex_send, ex_recv, ey_send, ey_recv, ez_send, ez_recv,
    xy_send, xy_recv, z_send, z_recv,
    above_send, above_recv, below_send, below_recv, row_send, row_recv, relay,
):
    cut = right.shape[2]
    half = cut // 2
    steps = half // STEP
    row, col = lax.axis_index("row"), lax.axis_index("col")
    x, y, hi = col % nx, col // nx % ny, col // (nx * ny)
    plane = nx * ny
    here = y * nx + x
    has_above, has_below = row > 0, row < rows_total - 1

    pairs = (
        (ham_hbm, ham), (par_hbm, par), (right, v_right), (left, v_left), (down, v_down), (up, v_up),
    )
    loads = [
        pltpu.make_async_copy(source, target, load_sem.at[i]) for i, (source, target) in enumerate(pairs)
    ]
    for load in loads:
        load.start()

    core, depth = row % 2, rows_total // 2
    z_count = 2 * depth
    z = hi * depth + row // 2

    def device(dx=0, dy=0, dz=0, other=False):
        at_z = (z + dz) % z_count
        place = (y + dy) % ny * nx + (x + dx) % nx
        return (at_z % depth * 2 + (1 - core if other else core), at_z // depth * plane + place)

    def signal(semaphore, target):
        pl.semaphore_signal(semaphore, inc=1, device_id=target, device_id_type=MESH)

    barrier = pltpu.get_barrier_semaphore()
    near = [device(dx=1), device(dx=-1), device(dy=1), device(dy=-1), device(other=True)]
    near += [device(dz=step, other=other) for step in (1, -1) for other in (False, True)]
    for target in near:
        signal(barrier, target)
    pl.semaphore_wait(barrier, len(near))
    for i, target in enumerate((device(dx=-1), device(dy=-1), device(dz=1), device(dz=-1))):
        signal(relay.at[i], target)

    def span(start):
        return pl.ds(pl.multiple_of(start, STEP), STEP)

    def send_down(i):
        at = span(i * STEP)
        return pltpu.make_async_remote_copy(
            down.at[:, :, at], from_above.at[:, :, at], down_send.at[i], down_recv.at[i],
            device_id=(row + 1, col), device_id_type=MESH,
        )

    def up_start(i):
        return (i * STEP + half) % cut

    def send_up(i):
        at = span(up_start(i))
        return pltpu.make_async_remote_copy(
            up.at[:, :, at], from_below.at[:, :, at], up_send.at[i], up_recv.at[i],
            device_id=(row - 1, col), device_id_type=MESH,
        )

    for i in range(steps):

        @pl.when(has_below)
        def _(i=i):
            send_down(i).start()

        @pl.when(has_above)
        def _(i=i):
            send_up(i).start()

    for load in loads[:2]:
        load.wait()
    tile = sign_tile(par).astype(BF16)
    sign[...] = jnp.concatenate([tile] * (STEP // 128), axis=1)
    coupling = lane_coupling(ham[...])

    def flat(ref, at):
        return ref[:, :, at].reshape(FLAT, STEP)

    def signed(ref, at):
        value = flat(ref, at) * sign[...]
        ref[:, :, at] = value.reshape(PAIRS, SITES, STEP)
        return value

    def product(first, second):
        return lax.dot_general(first, second, (((1,), (1,)), ((), ())), preferred_element_type=F32)

    for gram in (gram_h, gram_dd, gram_uu, gram_d, gram_u):
        gram[...] = jnp.zeros_like(gram)
    for load in loads[2:]:
        load.wait()

    @pl.loop(0, 2 * steps)
    def _(i):
        at = span(i * STEP)
        data = jnp.concatenate([flat(v_right, at), signed(v_left, at)], axis=0)
        gram_h[...] += product(data, data)
        data = flat(v_down, at)
        gram_dd[...] += product(data, data)
        data = signed(v_up, at)
        gram_uu[...] += product(data, data)

    def gather(value, buf, me, devices, send, recv):
        buf[me] = value
        copies = [
            pltpu.make_async_remote_copy(
                buf.at[me], buf.at[me], send.at[i], recv.at[me], device_id=device, device_id_type=MESH
            )
            for i, device in enumerate(devices)
        ]
        for copy in copies:
            copy.start()
        return copies

    def arrived(buf, slot, recv):
        pltpu.make_async_remote_copy(
            buf.at[slot], buf.at[slot], recv.at[slot], recv.at[slot], device_id=(row, col), device_id_type=MESH
        ).wait_recv()

    def all_arrived(buf, me, recv):
        count = buf.shape[0]
        for i in range(1, count):
            arrived(buf, (me + i) % count, recv)
        value = buf[0]
        for i in range(1, count):
            value = value + buf[i]
        return value

    early = compact(
        [gram_h[:FLAT, FLAT:], gram_h[:FLAT, :FLAT], gram_h[FLAT:, FLAT:], gram_dd[...], gram_uu[...]],
        [1, 0, 0, 0, 0],
    )
    early[2] = rolled(early[2], 1)
    for i in range(4):
        pl.semaphore_wait(relay.at[i], 1)
    for i, step in enumerate((2, -2)):
        signal(relay.at[4 + i], device(dz=step))
    same_x = [device(dx=i) for i in range(1, nx)]
    same_y = [device(dy=i) for i in range(1, ny)]
    offsets = [(i % nx, i // nx) for i in range(1, plane)]
    offsets.sort(key=lambda d: -min(d[0], nx - d[0]) - min(d[1], ny - d[1]))
    same_plane = [device(dx=dx, dy=dy) for dx, dy in offsets]
    sends = gather(jnp.concatenate(early, axis=1), early_x, x, same_x, ex_send, ex_recv)

    def meet(i):
        at, at_up = span(i * STEP), span(up_start(i))

        @pl.when(has_above)
        def _():
            send_down(i).wait_recv()
            gram_u[...] += product(flat(from_above, at), flat(v_up, at))

        @pl.when(has_below)
        def _():
            send_up(i).wait_recv()
            gram_d[...] += product(flat(v_down, at_up), signed(from_below, at_up))
            send_down(i).wait_send()
            send_down(i + steps).start()

        @pl.when(has_above)
        def _():
            send_up(i).wait_send()
            send_up(i + steps).start()

    for i in range(steps // 2):
        meet(i)
    early = all_arrived(early_x, x, ex_recv)
    sends += gather(early, early_y, y, same_y, ey_send, ey_recv)
    for i in range(steps // 2, steps):
        meet(i)

    late = jnp.concatenate(compact([gram_d[...], gram_u[...]], [0, 0]), axis=1)
    sends += gather(late, late_xy, here, same_plane, xy_send, xy_recv)
    early = all_arrived(early_y, y, ey_recv)
    for i in (4, 5):
        pl.semaphore_wait(relay.at[i], 1)
    partner = device(dz=depth)
    sends += gather(early, early_z, hi, [partner], ez_send, ez_recv)
    late = all_arrived(late_xy, here, xy_recv)

    sends += gather(late, late_z, hi, [partner], z_send, z_recv)

    def to_below(z):
        return pltpu.make_async_remote_copy(
            late_z.at[hi, :, pl.ds(0, LANES)], late_above.at[hi],
            below_send.at[z], above_recv.at[hi], device_id=(row + 1, z * plane + here), device_id_type=MESH,
        )

    def to_above(z):
        return pltpu.make_async_remote_copy(
            late_z.at[hi, :, pl.ds(LANES, LANES)], late_below.at[hi],
            above_send.at[z], below_recv.at[hi], device_id=(row - 1, z * plane + here), device_id_type=MESH,
        )

    @pl.when(has_below)
    def _():
        for z in (0, 1):
            to_below(z).start()

    @pl.when(has_above)
    def _():
        for z in (0, 1):
            to_above(z).start()

    early = all_arrived(early_z, hi, ez_recv)
    density_h, rr, ll, dd, uu = [early[:, i * LANES : (i + 1) * LANES] for i in range(5)]
    rr, ll, dd, uu = [thirds(block(g, 0, False, True)) for g in (rr, ll, dd, uu)]
    site = iota((SITES, 1), 0).astype(F32)
    weight = 1.0 + 2.0 * site / SITES + row.astype(F32) / rows_total
    weight_above = 1.0 + 2.0 * site / SITES + (row - 1).astype(F32) / rows_total
    energy_h, lam_h = finish(density_h, coupling, jnp.where(site < SITES - 1, weight, 0.0))
    weights = block(lam_h, 0, False, False)
    small = weights.astype(BF16)
    total_h = sum(dot16(small, g) for g in ll) + sum(dot16(g, small) for g in rr)
    square_h = (total_h * weights).sum()
    to_right = block(lam_h, 1, False, False).astype(BF16)
    to_left = block(lam_h, 1, True, False).astype(BF16)

    def put(ref, at, value):
        ref[:, :, at] = value.reshape(PAIRS, SITES, STEP)

    def grads_h(first, last):
        @pl.loop(first, last)
        def _(i):
            at = span(i * STEP)
            put(g_right, at, dot16(to_right, flat(v_left, at)))
            put(g_left, at, dot16(to_left, flat(v_right, at)) * sign[...].astype(F32))

    grads_h(0, steps)
    late = all_arrived(late_z, hi, z_recv)

    @pl.when(has_above)
    def _():
        for z in (0, 1):
            arrived(late_above, z, above_recv)

    @pl.when(has_below)
    def _():
        for z in (0, 1):
            arrived(late_below, z, below_recv)

    @pl.when(jnp.logical_not(has_above))
    def _():
        late_above[...] = jnp.zeros_like(late_above)

    @pl.when(jnp.logical_not(has_below))
    def _():
        late_below[...] = jnp.zeros_like(late_below)

    density_v = late[:, :LANES] + (late_below[0] + late_below[1])
    density_w = (late_above[0] + late_above[1]) + late[:, LANES:]
    energy_v, lam_v = finish(density_v, coupling, weight * has_below.astype(F32))
    _, lam_w = finish(density_w, coupling, weight_above * has_above.astype(F32))
    weights_v, weights_w = block(lam_v, 0, False, False), block(lam_w, 0, False, False)
    to_down, small = weights_v.astype(BF16), weights_w.astype(BF16)
    total_v = sum(dot16(g, to_down) for g in dd)
    total_w = sum(dot16(small, g) for g in uu)
    square = square_h + (total_v * weights_v + total_w * weights_w).sum()
    energies = (energy_h + energy_v).sum()
    lane = iota((SITES, LANES), 1)
    message = jnp.where(lane == 0, square, jnp.where(lane == 1, energies, 0.0))
    mates = [device(dz=step, other=other) for step in (0, 1, -1, 2) for other in (False, True)][1:]
    sends += gather(message, buf_row, row, mates, row_send, row_recv)
    to_up = block(lam_w, 0, True, False).astype(BF16)
    grads_h(steps, 2 * steps)

    @pl.loop(0, 2 * steps)
    def _(i):
        at, at_up = span(i * STEP), span(up_start(i))

        @pl.when(has_above)
        def _():
            @pl.when(i >= steps)
            def _():
                send_down(i).wait_recv()

            put(g_up, at, dot16(to_up, flat(from_above, at)) * sign[...].astype(F32))

        @pl.when(has_below)
        def _():
            @pl.when(i >= steps)
            def _():
                send_up(i).wait_recv()
                signed(from_below, at_up)

            put(g_down, at_up, dot16(to_down, flat(from_below, at_up)))

    @pl.when(jnp.logical_not(has_above))
    def _():
        g_up[...] = jnp.zeros_like(g_up)

    @pl.when(jnp.logical_not(has_below))
    def _():
        g_down[...] = jnp.zeros_like(g_down)

    @pl.when(has_below)
    def _():
        for i in range(steps, 2 * steps):
            send_down(i).wait_send()
        for z in (0, 1):
            to_below(z).wait_send()

    @pl.when(has_above)
    def _():
        for i in range(steps, 2 * steps):
            send_up(i).wait_send()
        for z in (0, 1):
            to_above(z).wait_send()

    totals[...] = all_arrived(buf_row, row, row_recv)
    for copy in sends:
        copy.wait_send()


def scale_kernel(
    count, totals, raw_right, raw_left, raw_down, raw_up,
    g_right, g_left, g_down, g_up, energy, o_right, o_left, o_down, o_up, o_energy, sems, energy_sem,
):
    message = totals[...]
    square = jnp.maximum(message[:1, :1], 0.0)
    scale = 1.0 / jnp.sqrt(square / count + 1e-06)
    o_energy[...] = message[:1, 1:2] / SITES
    copies = [pltpu.make_async_copy(o_energy, energy, energy_sem)]
    copies[0].start()
    arrays = (
        (raw_right, o_right, g_right), (raw_left, o_left, g_left), (raw_down, o_down, g_down), (raw_up, o_up, g_up),
    )
    for a, (raw, out, target) in enumerate(arrays):
        for p in range(PAIRS):

            @pl.loop(0, raw.shape[2] // STEP, unroll=True)
            def _(i, p=p, raw=raw, out=out):
                at = pl.ds(pl.multiple_of(i * STEP, STEP), STEP)
                out[p, :, at] = (raw[p, :, at] * scale).astype(BF16)

            copies.append(pltpu.make_async_copy(out.at[p], target.at[p], sems.at[a, p]))
            copies[-1].start()
    for copy in copies:
        copy.wait()


def shards(nx, ny, cols_total, right_env, left_env, down_env, up_env, hamiltonian, parity):
    rows_total = lax.axis_size("row")
    cut = right_env.shape[3]
    chunks = cut // STEP
    envs = [e.transpose(0, 2, 1, 3).reshape(PAIRS, SITES, cut) for e in (right_env, left_env, down_env, up_env)]
    env = (PAIRS, SITES, cut)
    dma = pltpu.SemaphoreType.DMA
    hbm_spec = pl.BlockSpec(memory_space=pltpu.HBM)
    vmem_spec = pl.BlockSpec(memory_space=pltpu.VMEM)
    square = pltpu.VMEM((FLAT, FLAT), F32)
    early, late = 5 * LANES, 2 * LANES
    raw = pl.pallas_call(
        functools.partial(kernel, nx, ny, rows_total),
        out_shape=[pltpu.VMEM(env, F32)] * 4 + [pltpu.VMEM((SITES, LANES), F32)],
        in_specs=[hbm_spec] * 6,
        out_specs=[vmem_spec] * 5,
        scratch_shapes=[pltpu.VMEM(env, BF16)] * 6
        + [
            pltpu.VMEM((PAIRS, PAIRS), F32),
            pltpu.SMEM((BOND,), jnp.int32),
            pltpu.VMEM((FLAT, STEP), BF16),
            pltpu.VMEM((2 * FLAT, 2 * FLAT), F32),
            square, square, square, square,
            pltpu.VMEM((nx, SITES, early), F32),
            pltpu.VMEM((ny, SITES, early), F32),
            pltpu.VMEM((2, SITES, early), F32),
            pltpu.VMEM((nx * ny, SITES, late), F32),
            pltpu.VMEM((2, SITES, late), F32),
            pltpu.VMEM((2, SITES, LANES), F32),
            pltpu.VMEM((2, SITES, LANES), F32),
            pltpu.VMEM((rows_total, SITES, LANES), F32),
            dma((6,)),
            dma((chunks,)), dma((chunks,)), dma((chunks,)), dma((chunks,)),
            dma((nx,)), dma((nx,)), dma((ny,)), dma((ny,)), dma((2,)), dma((2,)),
            dma((nx * ny,)), dma((nx * ny,)), dma((2,)), dma((2,)),
            dma((2,)), dma((2,)), dma((2,)), dma((2,)), dma((rows_total,)), dma((rows_total,)),
            pltpu.SemaphoreType.REGULAR((6,)),
        ],
        compiler_params=pltpu.CompilerParams(
            collective_id=0, has_side_effects=True, vmem_limit_bytes=32 * 1024 * 1024
        ),
    )(*[pltpu.with_memory_space_constraint(a, pltpu.HBM) for a in (*envs, hamiltonian, parity)])
    count = 4.0 * rows_total * FLAT * cols_total * cut
    outs = pl.pallas_call(
        functools.partial(scale_kernel, count),
        out_shape=[jax.ShapeDtypeStruct(env, BF16)] * 4 + [jax.ShapeDtypeStruct((1, 1), F32)],
        in_specs=[vmem_spec] * 5,
        out_specs=[hbm_spec] * 5,
        scratch_shapes=[pltpu.VMEM(env, BF16)] * 4 + [pltpu.VMEM((1, 1), F32), dma((4, PAIRS)), dma],
        compiler_params=pltpu.CompilerParams(vmem_limit_bytes=16 * 1024 * 1024),
    )(*[pltpu.with_memory_space_constraint(a, pltpu.VMEM) for a in (raw[4], *raw[:4])])
    grads = [g.reshape(1, PAIRS, SITES, cut).transpose(0, 2, 1, 3) for g in outs[:4]]
    return (*grads, outs[4].reshape(()))


def solution(mesh):
    spec = P("row", None, None, "col")
    side = 4
    return jax.shard_map(
        functools.partial(shards, side, mesh.shape["col"] // (2 * side), mesh.shape["col"]),
        mesh=mesh,
        in_specs=(spec, spec, spec, spec, P(), P()),
        out_specs=(spec, spec, spec, spec, P()),
        check_vma=False,
    )
```

```python
import functools

import jax
import jax.numpy as jnp
from jax import lax
from jax.experimental import pallas as pl
from jax.experimental.pallas import tpu as pltpu
from jax.sharding import PartitionSpec as P

PAIRS = 9
SITES = 8
FLAT = PAIRS * SITES
BOND = 8
LANES = 128
STEP = 2048
MESH = pl.DeviceIdType.MESH
HIGHEST = lax.Precision.HIGHEST
F32 = jnp.float32
BF16 = jnp.bfloat16


def iota(shape, dim):
    return lax.broadcasted_iota(jnp.int32, shape, dim)


def dot32(a, b):
    return jnp.dot(a, b, precision=HIGHEST, preferred_element_type=F32)


def dot16(a, b):
    return jnp.dot(a, b, preferred_element_type=F32)


def sign_tile(par):
    shape = (FLAT, 128)
    pair = iota(shape, 0) // SITES
    lane = iota(shape, 1) % (BOND * BOND)
    ket, bra = lane // BOND, lane % BOND
    par_ket = jnp.zeros(shape, jnp.int32)
    par_bra = jnp.zeros(shape, jnp.int32)
    for bond in range(BOND):
        value = par[bond]
        par_ket = jnp.where(ket == bond, value, par_ket)
        par_bra = jnp.where(bra == bond, value, par_bra)
    exponent = jnp.minimum(pair // 3, 1) * par_ket + jnp.minimum(pair % 3, 1) * par_bra
    return (1 - 2 * (exponent % 2)).astype(F32)


def compact(grams, shifts):
    square = (FLAT, FLAT)
    row_site, col_site = iota(square, 0) % SITES, iota(square, 1) % SITES
    rows = jnp.concatenate(
        [jnp.where(col_site == row_site + shift, gram, 0.0) for gram, shift in zip(grams, shifts, strict=True)],
        axis=0,
    )
    spread = (FLAT, LANES)
    source, lane = iota(spread, 0), iota(spread, 1)
    wide = dot32(rows, (lane % PAIRS == source // SITES).astype(F32))
    keep = lane // PAIRS == source // SITES
    out = []
    for i in range(len(grams)):
        part = jnp.where(keep, wide[i * FLAT : (i + 1) * FLAT], 0.0)
        out.append(part.reshape(PAIRS, SITES, LANES).sum(axis=0))
    return out


def rolled(rows, shift):
    shift %= SITES
    if not shift:
        return rows
    return jnp.concatenate([rows[shift:], rows[:shift]], axis=0)


def lane_coupling(ham):
    shape = (PAIRS, PAIRS)
    p, q = iota(shape, 0), iota(shape, 1)

    def charge(state):
        return jnp.minimum(state, 1)

    same = charge(p // 3) + charge(q // 3) == charge(p % 3) + charge(q % 3)
    coupling = jnp.where(same, ham, 0.0)
    shape = (PAIRS, LANES)
    row, lane = iota(shape, 0), iota(shape, 1)
    wide = dot32(coupling, (lane % PAIRS == row).astype(F32))
    return jnp.where(lane // PAIRS == row, wide, 0.0).sum(axis=0, keepdims=True)


def finish(density, coupling, factor):
    entries = PAIRS * PAIRS
    norm = jnp.sqrt((density * density).sum(axis=1, keepdims=True) / entries + 1e-06)
    trace = (coupling * density).sum(axis=1, keepdims=True)
    energy = factor * trace / norm
    lam = factor * (coupling / norm - trace / (entries * norm**3) * density)
    return energy, lam.astype(BF16).astype(F32)


def block(rows, shift, transposed, exact):
    shape = (FLAT, LANES)
    row, lane = iota(shape, 0), iota(shape, 1)
    tall = jnp.concatenate([rolled(rows, -shift) if transposed else rows] * PAIRS, axis=0)
    mine = lane % PAIRS if transposed else lane // PAIRS
    tall = jnp.where(mine == row // SITES, tall, 0.0)
    shape = (LANES, FLAT)
    source, col = iota(shape, 0), iota(shape, 1)
    other = source // PAIRS if transposed else source % PAIRS
    pick = (other == col // SITES).astype(F32)
    wide = dot32(tall, pick) if exact else dot16(tall.astype(BF16), pick.astype(BF16))
    shape = (FLAT, FLAT)
    row_site, col_site = iota(shape, 0) % SITES, iota(shape, 1) % SITES
    hit = row_site == col_site + shift if transposed else col_site == row_site + shift
    return jnp.where(hit, wide, 0.0)


def thirds(value):
    high = value.astype(BF16)
    rest = value - high.astype(F32)
    middle = rest.astype(BF16)
    return high, middle, (rest - middle.astype(F32)).astype(BF16)


def kernel(
    nx, ny, rows_total,
    right, left, down, up, ham_hbm, par_hbm,
    g_right, g_left, g_down, g_up, totals,
    v_right, v_left, v_down, v_up, from_above, from_below, ham, par, sign,
    gram_h, gram_dd, gram_uu, gram_d, gram_u, early_x, early_y, early_z, late_xy, late_z,
    late_above, late_below, buf_row,
    load_sem, down_send, down_recv, up_send, up_recv,
    ex_send, ex_recv, ey_send, ey_recv, ez_send, ez_recv,
    xy_send, xy_recv, z_send, z_recv,
    above_send, above_recv, below_send, below_recv, row_send, row_recv, relay,
):
    cut = right.shape[2]
    half = cut // 2
    steps = half // STEP
    row, col = lax.axis_index("row"), lax.axis_index("col")
    x, y, hi = col % nx, col // nx % ny, col // (nx * ny)
    plane = nx * ny
    here = y * nx + x
    has_above, has_below = row > 0, row < rows_total - 1
    row_above, row_below = (row - 1) % rows_total, (row + 1) % rows_total

    pairs = (
        (ham_hbm, ham), (par_hbm, par), (right, v_right), (left, v_left), (down, v_down), (up, v_up),
    )
    loads = [
        pltpu.make_async_copy(source, target, load_sem.at[i]) for i, (source, target) in enumerate(pairs)
    ]
    for load in loads:
        load.start()

    core, depth = row % 2, rows_total // 2
    z_count = 2 * depth
    z = hi * depth + row // 2

    def device(dx=0, dy=0, dz=0, other=False):
        at_z = (z + dz) % z_count
        place = (y + dy) % ny * nx + (x + dx) % nx
        return (at_z % depth * 2 + (1 - core if other else core), at_z // depth * plane + place)

    def signal(semaphore, target):
        pl.semaphore_signal(semaphore, inc=1, device_id=target, device_id_type=MESH)

    barrier = pltpu.get_barrier_semaphore()
    near = [device(dx=1), device(dx=-1), device(dy=1), device(dy=-1), device(other=True)]
    near += [device(dz=step, other=other) for step in (1, -1) for other in (False, True)]
    for target in near:
        signal(barrier, target)
    pl.semaphore_wait(barrier, len(near))
    for i, target in enumerate((device(dx=-1), device(dy=-1), device(dz=1), device(dz=-1))):
        signal(relay.at[i], target)

    def span(start):
        return pl.ds(pl.multiple_of(start, STEP), STEP)

    def send_down(i):
        at = span(i * STEP)
        return pltpu.make_async_remote_copy(
            down.at[:, :, at], from_above.at[:, :, at], down_send.at[i], down_recv.at[i],
            device_id=(row_below, col), device_id_type=MESH,
        )

    def up_start(i):
        return (i * STEP + half) % cut

    def send_up(i):
        at = span(up_start(i))
        return pltpu.make_async_remote_copy(
            up.at[:, :, at], from_below.at[:, :, at], up_send.at[i], up_recv.at[i],
            device_id=(row_above, col), device_id_type=MESH,
        )

    for i in range(steps):

        @pl.when(has_below)
        def _(i=i):
            send_down(i).start()

        @pl.when(has_above)
        def _(i=i):
            send_up(i).start()

    for load in loads[:2]:
        load.wait()
    tile = sign_tile(par).astype(BF16)
    sign[...] = jnp.concatenate([tile] * (STEP // 128), axis=1)
    coupling = lane_coupling(ham[...])

    def flat(ref, at):
        return ref[:, :, at].reshape(FLAT, STEP)

    def signed(ref, at):
        value = flat(ref, at) * sign[...]
        ref[:, :, at] = value.reshape(PAIRS, SITES, STEP)
        return value

    def product(first, second):
        return lax.dot_general(first, second, (((1,), (1,)), ((), ())), preferred_element_type=F32)

    for gram in (gram_h, gram_dd, gram_uu, gram_d, gram_u):
        gram[...] = jnp.zeros_like(gram)
    for load in loads[2:]:
        load.wait()

    @pl.loop(0, 2 * steps)
    def _(i):
        at = span(i * STEP)
        data = jnp.concatenate([flat(v_right, at), signed(v_left, at)], axis=0)
        gram_h[...] += product(data, data)
        data = flat(v_down, at)
        gram_dd[...] += product(data, data)
        data = signed(v_up, at)
        gram_uu[...] += product(data, data)

    def gather(value, buf, me, devices, send, recv):
        buf[me] = value
        copies = [
            pltpu.make_async_remote_copy(
                buf.at[me], buf.at[me], send.at[i], recv.at[me], device_id=device, device_id_type=MESH
            )
            for i, device in enumerate(devices)
        ]
        for copy in copies:
            copy.start()
        return copies

    def arrived(buf, slot, recv):
        pltpu.make_async_remote_copy(
            buf.at[slot], buf.at[slot], recv.at[slot], recv.at[slot], device_id=(row, col), device_id_type=MESH
        ).wait_recv()

    def all_arrived(buf, me, recv):
        count = buf.shape[0]
        for i in range(1, count):
            arrived(buf, (me + i) % count, recv)
        value = buf[0]
        for i in range(1, count):
            value = value + buf[i]
        return value

    early = compact(
        [gram_h[:FLAT, FLAT:], gram_h[:FLAT, :FLAT], gram_h[FLAT:, FLAT:], gram_dd[...], gram_uu[...]],
        [1, 0, 0, 0, 0],
    )
    early[2] = rolled(early[2], 1)
    for i in range(4):
        pl.semaphore_wait(relay.at[i], 1)
    for i, step in enumerate((2, -2)):
        signal(relay.at[4 + i], device(dz=step))
    same_x = [device(dx=i) for i in range(1, nx)]
    same_y = [device(dy=i) for i in range(1, ny)]
    offsets = [(i % nx, i // nx) for i in range(1, plane)]
    offsets.sort(key=lambda d: -min(d[0], nx - d[0]) - min(d[1], ny - d[1]))
    same_plane = [device(dx=dx, dy=dy) for dx, dy in offsets]
    sends = gather(jnp.concatenate(early, axis=1), early_x, x, same_x, ex_send, ex_recv)

    def meet(i):
        at, at_up = span(i * STEP), span(up_start(i))

        @pl.when(has_above)
        def _():
            send_down(i).wait_recv()
            gram_u[...] += product(flat(from_above, at), flat(v_up, at))

        @pl.when(has_below)
        def _():
            send_up(i).wait_recv()
            gram_d[...] += product(flat(v_down, at_up), signed(from_below, at_up))
            send_down(i).wait_send()
            send_down(i + steps).start()

        @pl.when(has_above)
        def _():
            send_up(i).wait_send()
            send_up(i + steps).start()

    for i in range(steps // 2):
        meet(i)
    early = all_arrived(early_x, x, ex_recv)
    sends += gather(early, early_y, y, same_y, ey_send, ey_recv)
    for i in range(steps // 2, steps):
        meet(i)

    late = jnp.concatenate(compact([gram_d[...], gram_u[...]], [0, 0]), axis=1)
    sends += gather(late, late_xy, here, same_plane, xy_send, xy_recv)
    early = all_arrived(early_y, y, ey_recv)
    for i in (4, 5):
        pl.semaphore_wait(relay.at[i], 1)
    partner = device(dz=depth)
    sends += gather(early, early_z, hi, [partner], ez_send, ez_recv)
    late = all_arrived(late_xy, here, xy_recv)

    late_z[hi] = late

    def to_below(z):
        return pltpu.make_async_remote_copy(
            late_z.at[hi, :, pl.ds(0, LANES)], late_above.at[hi],
            below_send.at[z], above_recv.at[hi], device_id=(row_below, z * plane + here), device_id_type=MESH,
        )

    def to_above(z):
        return pltpu.make_async_remote_copy(
            late_z.at[hi, :, pl.ds(LANES, LANES)], late_below.at[hi],
            above_send.at[z], below_recv.at[hi], device_id=(row_above, z * plane + here), device_id_type=MESH,
        )

    @pl.when(has_below)
    def _():
        for z in (0, 1):
            to_below(z).start()

    @pl.when(has_above)
    def _():
        for z in (0, 1):
            to_above(z).start()

    sends.append(
        pltpu.make_async_remote_copy(
            late_z.at[hi], late_z.at[hi], z_send.at[0], z_recv.at[hi], device_id=partner, device_id_type=MESH
        )
    )
    sends[-1].start()

    early = all_arrived(early_z, hi, ez_recv)
    density_h, rr, ll, dd, uu = [early[:, i * LANES : (i + 1) * LANES] for i in range(5)]
    rr, ll, dd, uu = [thirds(block(g, 0, False, True)) for g in (rr, ll, dd, uu)]
    site = iota((SITES, 1), 0).astype(F32)
    weight = 1.0 + 2.0 * site / SITES + row.astype(F32) / rows_total
    weight_above = 1.0 + 2.0 * site / SITES + (row - 1).astype(F32) / rows_total
    energy_h, lam_h = finish(density_h, coupling, jnp.where(site < SITES - 1, weight, 0.0))
    weights = block(lam_h, 0, False, False)
    small = weights.astype(BF16)
    total_h = sum(dot16(small, g) for g in ll) + sum(dot16(g, small) for g in rr)
    square_h = (total_h * weights).sum()
    to_right = block(lam_h, 1, False, False).astype(BF16)
    to_left = block(lam_h, 1, True, False).astype(BF16)

    def put(ref, at, value):
        ref[:, :, at] = value.reshape(PAIRS, SITES, STEP)

    def grads_h(first, last):
        @pl.loop(first, last)
        def _(i):
            at = span(i * STEP)
            put(g_right, at, dot16(to_right, flat(v_left, at)))
            put(g_left, at, dot16(to_left, flat(v_right, at)) * sign[...].astype(F32))

    grads_h(0, steps)
    late = all_arrived(late_z, hi, z_recv)

    @pl.when(has_above)
    def _():
        for z in (0, 1):
            arrived(late_above, z, above_recv)

    @pl.when(has_below)
    def _():
        for z in (0, 1):
            arrived(late_below, z, below_recv)

    @pl.when(jnp.logical_not(has_above))
    def _():
        late_above[...] = jnp.zeros_like(late_above)

    @pl.when(jnp.logical_not(has_below))
    def _():
        late_below[...] = jnp.zeros_like(late_below)

    density_v = late[:, :LANES] + (late_below[0] + late_below[1])
    density_w = (late_above[0] + late_above[1]) + late[:, LANES:]
    energy_v, lam_v = finish(density_v, coupling, weight * has_below.astype(F32))
    _, lam_w = finish(density_w, coupling, weight_above * has_above.astype(F32))
    weights_v, weights_w = block(lam_v, 0, False, False), block(lam_w, 0, False, False)
    to_down, small = weights_v.astype(BF16), weights_w.astype(BF16)
    total_v = sum(dot16(g, to_down) for g in dd)
    total_w = sum(dot16(small, g) for g in uu)
    square = square_h + (total_v * weights_v + total_w * weights_w).sum()
    energies = (energy_h + energy_v).sum()
    lane = iota((SITES, LANES), 1)
    message = jnp.where(lane == 0, square, jnp.where(lane == 1, energies, 0.0))
    mates = [device(dz=step, other=other) for step in (0, 1, -1, 2) for other in (False, True)][1:]
    sends += gather(message, buf_row, row, mates, row_send, row_recv)
    to_up = block(lam_w, 0, True, False).astype(BF16)
    grads_h(steps, 2 * steps)

    @pl.loop(0, 2 * steps)
    def _(i):
        at, at_up = span(i * STEP), span(up_start(i))

        @pl.when(has_above)
        def _():
            @pl.when(i >= steps)
            def _():
                send_down(i).wait_recv()

            put(g_up, at, dot16(to_up, flat(from_above, at)) * sign[...].astype(F32))

        @pl.when(has_below)
        def _():
            @pl.when(i >= steps)
            def _():
                send_up(i).wait_recv()
                signed(from_below, at_up)

            put(g_down, at_up, dot16(to_down, flat(from_below, at_up)))

    @pl.when(jnp.logical_not(has_above))
    def _():
        g_up[...] = jnp.zeros_like(g_up)

    @pl.when(jnp.logical_not(has_below))
    def _():
        g_down[...] = jnp.zeros_like(g_down)

    @pl.when(has_below)
    def _():
        for i in range(steps, 2 * steps):
            send_down(i).wait_send()
        for z in (0, 1):
            to_below(z).wait_send()

    @pl.when(has_above)
    def _():
        for i in range(steps, 2 * steps):
            send_up(i).wait_send()
        for z in (0, 1):
            to_above(z).wait_send()

    totals[...] = all_arrived(buf_row, row, row_recv)
    for copy in sends:
        copy.wait_send()


def scale_kernel(
    count, totals, raw_right, raw_left, raw_down, raw_up,
    g_right, g_left, g_down, g_up, energy, o_right, o_left, o_down, o_up, o_energy, sems, energy_sem,
):
    message = totals[...]
    square = jnp.maximum(message[:1, :1], 0.0)
    scale = 1.0 / jnp.sqrt(square / count + 1e-06)
    o_energy[...] = message[:1, 1:2] / SITES
    copies = [pltpu.make_async_copy(o_energy, energy, energy_sem)]
    copies[0].start()
    arrays = (
        (raw_right, o_right, g_right), (raw_left, o_left, g_left), (raw_down, o_down, g_down), (raw_up, o_up, g_up),
    )
    for a, (raw, out, target) in enumerate(arrays):
        for p in range(PAIRS):

            @pl.loop(0, raw.shape[2] // STEP, unroll=True)
            def _(i, p=p, raw=raw, out=out):
                at = pl.ds(pl.multiple_of(i * STEP, STEP), STEP)
                out[p, :, at] = (raw[p, :, at] * scale).astype(BF16)

            copies.append(pltpu.make_async_copy(out.at[p], target.at[p], sems.at[a, p]))
            copies[-1].start()
    for copy in copies:
        copy.wait()


def shards(nx, ny, cols_total, right_env, left_env, down_env, up_env, hamiltonian, parity):
    rows_total = lax.axis_size("row")
    cut = right_env.shape[3]
    chunks = cut // STEP
    envs = [e.transpose(0, 2, 1, 3).reshape(PAIRS, SITES, cut) for e in (right_env, left_env, down_env, up_env)]
    env = (PAIRS, SITES, cut)
    dma = pltpu.SemaphoreType.DMA
    hbm_spec = pl.BlockSpec(memory_space=pltpu.HBM)
    vmem_spec = pl.BlockSpec(memory_space=pltpu.VMEM)
    square = pltpu.VMEM((FLAT, FLAT), F32)
    early, late = 5 * LANES, 2 * LANES
    raw = pl.pallas_call(
        functools.partial(kernel, nx, ny, rows_total),
        out_shape=[pltpu.VMEM(env, F32)] * 4 + [pltpu.VMEM((SITES, LANES), F32)],
        in_specs=[hbm_spec] * 6,
        out_specs=[vmem_spec] * 5,
        scratch_shapes=[pltpu.VMEM(env, BF16)] * 6
        + [
            pltpu.VMEM((PAIRS, PAIRS), F32),
            pltpu.SMEM((BOND,), jnp.int32),
            pltpu.VMEM((FLAT, STEP), BF16),
            pltpu.VMEM((2 * FLAT, 2 * FLAT), F32),
            square, square, square, square,
            pltpu.VMEM((nx, SITES, early), F32),
            pltpu.VMEM((ny, SITES, early), F32),
            pltpu.VMEM((2, SITES, early), F32),
            pltpu.VMEM((nx * ny, SITES, late), F32),
            pltpu.VMEM((2, SITES, late), F32),
            pltpu.VMEM((2, SITES, LANES), F32),
            pltpu.VMEM((2, SITES, LANES), F32),
            pltpu.VMEM((rows_total, SITES, LANES), F32),
            dma((6,)),
            dma((chunks,)), dma((chunks,)), dma((chunks,)), dma((chunks,)),
            dma((nx,)), dma((nx,)), dma((ny,)), dma((ny,)), dma((2,)), dma((2,)),
            dma((nx * ny,)), dma((nx * ny,)), dma((2,)), dma((2,)),
            dma((2,)), dma((2,)), dma((2,)), dma((2,)), dma((rows_total,)), dma((rows_total,)),
            pltpu.SemaphoreType.REGULAR((6,)),
        ],
        compiler_params=pltpu.CompilerParams(
            collective_id=0, has_side_effects=True, vmem_limit_bytes=32 * 1024 * 1024
        ),
    )(*[pltpu.with_memory_space_constraint(a, pltpu.HBM) for a in (*envs, hamiltonian, parity)])
    count = 4.0 * rows_total * FLAT * cols_total * cut
    outs = pl.pallas_call(
        functools.partial(scale_kernel, count),
        out_shape=[jax.ShapeDtypeStruct(env, BF16)] * 4 + [jax.ShapeDtypeStruct((1, 1), F32)],
        in_specs=[vmem_spec] * 5,
        out_specs=[hbm_spec] * 5,
        scratch_shapes=[pltpu.VMEM(env, BF16)] * 4 + [pltpu.VMEM((1, 1), F32), dma((4, PAIRS)), dma],
        compiler_params=pltpu.CompilerParams(vmem_limit_bytes=16 * 1024 * 1024),
    )(*[pltpu.with_memory_space_constraint(a, pltpu.VMEM) for a in (raw[4], *raw[:4])])
    grads = [g.reshape(1, PAIRS, SITES, cut).transpose(0, 2, 1, 3) for g in outs[:4]]
    return (*grads, outs[4].reshape(()))


def solution(mesh):
    spec = P("row", None, None, "col")
    side = 4
    return jax.shard_map(
        functools.partial(shards, side, mesh.shape["col"] // (2 * side), mesh.shape["col"]),
        mesh=mesh,
        in_specs=(spec, spec, spec, spec, P(), P()),
        out_specs=(spec, spec, spec, spec, P()),
        check_vma=False,
    )
```
